32 devices in a mesh: col: 8 (over z, x), rep: 4 (over y, core).
Axes of the slice: x: 2, y: 2, z: 4, core: 2. Of those that a mesh axis runs over, the one named last changes fastest.
Arguments:
- coords: bfloat16 [65536, 128], P(('col', 'rep')), may hold values from -6 to 6
- dissim: bfloat16 [32, 5, 64, 128, 128], P(('col', 'rep')), may hold values from 8 to 24
- tile_blocks: int32 [32, 5, 64, 2], P(('col', 'rep')), may hold values from 0 to 63, as said below
- tile_count: int32 [32, 5], P(('col', 'rep')), may hold values from 8 to 64, as said below
Outputs:
- updated: float32 [65536, 128], P(('col', 'rep'))
The draws below stay inside these ranges and needn't reach their ends.
Inputs may be any that keep to these rules, and one draw needn't show every extreme that they name: `tile_blocks`: within one list and offset no (row block, column block) pair repeats; slots at or past the live count are ignored. `tile_count`: A list has equally many live slots at every offset; some list has 64 at every offset.
All inputs are finite; a program needn't handle non-finite values.
Results may differ from the reference program's by a relative error of at most 0.0003.
Values may be sent and summed in bfloat16 or wider, within the bound.
No kernel may reach another device: no remote copies, remote signals or barrier semaphores. Data moves between devices by JAX's collectives and lax.ppermute only.
A program may use at most 128 MiB of HBM per device.

```python
import jax
import jax.numpy as jnp
from jax import lax

DIM = 128
BLK = 128
OFFSETS = 5
MAXT = 64
SHARDS = 8
STRIDE = 1
LISTS = 32
BLOCKS = 64
POINTS = 65536


def draw_tile_count(key, part):
    key = jax.random.fold_in(key, 11)
    first_key, second_key = jax.random.split(key)
    shifts = jax.random.randint(first_key, (LISTS,), 0, 4)
    chosen = jax.random.randint(second_key, (), 0, LISTS)
    shifts = jnp.where(jnp.arange(LISTS) == chosen, 0, shifts)
    counts = jnp.maximum(MAXT // jnp.left_shift(1, shifts), 1)
    return jnp.broadcast_to(counts[:, None], (LISTS, OFFSETS)).astype(jnp.int32)


def pick_pairs(one_key):
    return jax.random.permutation(one_key, BLOCKS * BLOCKS)[:MAXT]


def draw_tile_blocks(key, part):
    key = jax.random.fold_in(key, 23)
    many_keys = jax.random.split(key, LISTS * OFFSETS)
    picked = jax.vmap(pick_pairs)(many_keys)
    joined = jnp.stack([picked // BLOCKS, picked % BLOCKS], axis=-1)
    return joined.reshape(LISTS, OFFSETS, MAXT, 2).astype(jnp.int32)


def steps_of(stream_key, shape, shards, smallest, largest):
    def one(axis_at, blocks):
        steps = jax.random.uniform(jax.random.fold_in(jax.random.fold_in(stream_key, 6), axis_at), (blocks,), jnp.float32, smallest / len(shards), largest / len(shards))
        return jnp.repeat(jnp.exp(steps), shape[axis_at] // blocks).reshape((-1,) + (1,) * (len(shape) - axis_at - 1))

    level = one(*shards[0])
    for cut in shards[1:]:
        level = level * one(*cut)
    return level


def bell_draw(own_key, extent, width, most, cuts=(), held_as=jnp.bfloat16):
    entries = jax.random.normal(own_key, extent, jnp.float32) * width
    if len(cuts) > 0:
        entries = steps_of(own_key, extent, cuts, -0.22, 0.18) * entries
    return jnp.clip(entries, min=-most, max=most).astype(held_as)


def setup_inputs(seed: int = 0) -> dict:
    splits = jax.random.split(jax.random.key(seed), 5)
    coords = bell_draw(splits[0], (POINTS, DIM), 1.0, 6.0, ((0, 32),))
    dissim = jnp.clip(8.0 + 16.0 * jax.random.uniform(splits[1], (LISTS, OFFSETS, MAXT, BLK, BLK), jnp.float32) ** steps_of(splits[1], (LISTS, OFFSETS, MAXT, BLK, BLK), ((0, 32),), -0.2, 0.2), 8.0, 24.0).astype(jnp.bfloat16)
    tile_blocks = draw_tile_blocks(jax.random.fold_in(splits[4], 71), 0)
    tile_count = draw_tile_count(jax.random.fold_in(splits[4], 71), 0)
    return dict(coords=coords, dissim=dissim, tile_blocks=tile_blocks, tile_count=tile_count)


def tile_terms(left_rows, right_rows, left_norms, right_norms, targets, active):
    products = jnp.einsum('tid,tjd->tij', left_rows.astype(jnp.float32), right_rows.astype(jnp.float32))
    spacing = jnp.sqrt(left_norms[:, :, None] + right_norms[:, None, :] - 2.0 * products + 1.0)
    wanted = targets.astype(jnp.float32)
    weights = (16.0 / wanted) ** 2 * active
    rounded = lax.optimization_barrier((weights * (1.0 - wanted / spacing)).astype(jnp.bfloat16))
    ratios = rounded.astype(jnp.float32)
    pulled = jnp.einsum('tij,tjd->tid', ratios, right_rows.astype(jnp.float32))
    return (pulled, lax.optimization_barrier(jnp.sum(ratios, axis=-1)), lax.optimization_barrier(jnp.sum(weights, axis=-1)))

def reference(coords, dissim, tile_blocks, tile_count):
    per_group = LISTS // SHARDS
    all_blocks = coords.reshape(POINTS // BLK, BLK, DIM)
    points32 = coords.astype(jnp.float32)
    block_norms = lax.optimization_barrier(jnp.sum(points32 * points32, axis=-1)).reshape(POINTS // BLK, BLK)
    offsets = jnp.arange(OFFSETS, dtype=jnp.int32)
    slot_ids = jnp.arange(MAXT, dtype=jnp.int32)

    def visit(state, inputs):
        pulled, ratio_sum, weight_sum = state
        list_id, targets, tile_pairs, counts = inputs
        row_group = list_id // per_group
        source = (row_group - offsets * STRIDE) % SHARDS
        row_ids = (row_group * BLOCKS + tile_pairs[:, :, 0]).reshape(-1).astype(jnp.int32)
        col_ids = (source[:, None] * BLOCKS + tile_pairs[:, :, 1]).reshape(-1).astype(jnp.int32)
        active = (slot_ids[None, :] < counts[:, None]).reshape(-1, 1, 1).astype(jnp.float32)
        found = tile_terms(all_blocks[row_ids], all_blocks[col_ids], block_norms[row_ids], block_norms[col_ids], targets.reshape(-1, BLK, BLK), active)
        return ((pulled.at[row_ids].add(found[0]), ratio_sum.at[row_ids].add(found[1]), weight_sum.at[row_ids].add(found[2])), None)
    start = (jnp.zeros((POINTS // BLK, BLK, DIM), jnp.float32), jnp.zeros((POINTS // BLK, BLK), jnp.float32), jnp.zeros((POINTS // BLK, BLK), jnp.float32))
    (pulled, ratio_sum, weight_sum), _ = lax.scan(visit, start, (jnp.arange(LISTS, dtype=jnp.int32), dissim, tile_blocks, tile_count))
    pulled = pulled.reshape(POINTS, DIM)
    ratio_sum = ratio_sum.reshape(POINTS, 1)
    weight_sum = weight_sum.reshape(POINTS, 1)
    return points32 - (ratio_sum * points32 - pulled) / (weight_sum + 256.0)
```

```python
import functools

import jax
import jax.numpy as jnp
from jax import lax
from jax.experimental import pallas as pl
from jax.experimental.pallas import tpu as pltpu
from jax.sharding import PartitionSpec as P

GROUP = 4
PARAMS = pltpu.CompilerParams(vmem_limit_bytes=40 * 1024 * 1024)
VMEM, SMEM, HBM = pltpu.VMEM, pltpu.SMEM, pltpu.HBM


def lanes_of(shape):
    return lax.broadcasted_iota(jnp.int32, shape, len(shape) - 1)


def split_three(value):
    high = value.astype(jnp.bfloat16)
    rest = value - high.astype(jnp.float32)
    middle = rest.astype(jnp.bfloat16)
    low = (rest - middle.astype(jnp.float32)).astype(jnp.bfloat16)
    return high, middle, low


def norm_columns(points32, plus, first):
    norms = jnp.sum(points32 * points32, axis=-1, keepdims=True) + plus
    lanes = lanes_of(points32.shape)
    columns = jnp.where((lanes >= 3 - first) & (lanes < 6 - first), 1.0, 0.0)
    for place, part in enumerate(split_three(norms)):
        columns = jnp.where(lanes == first + place, part.astype(jnp.float32), columns)
    return columns.astype(jnp.bfloat16)


def row_vector(column_block):
    pick = jnp.where(lanes_of((8, column_block.shape[-1])) == 0, 1.0, 0.0)
    return lax.dot_general(
        pick,
        column_block,
        (((1,), (1,)), ((), ())),
        precision=lax.Precision.HIGHEST,
        preferred_element_type=jnp.float32,
    )[0:1]


def column_vector(row, side):
    eye = lax.broadcasted_iota(jnp.int32, (side, side), 0) == lanes_of((side, side))
    return jnp.sum(jnp.where(eye, row, 0.0), axis=1, keepdims=True)


def lists_kernel(slots, place, own, other, out):
    core, mine = place[0] % 2, place[0] // 2
    pieces, room = out.shape[0], out.shape[1]
    offsets = pieces // 2
    per_quarter = place[1]
    for piece in range(pieces):
        out[piece, 0] = 0

    for offset in range(offsets):
        for source, codes in enumerate((own, other)):

            def visit(slot, carry, offset=offset, source=source, codes=codes):
                code = codes[offset * slots + slot]
                row, col = code // 256, code % 256
                quarter = col // per_quarter
                piece = 2 * offset + jnp.where(quarter // 2 == mine, 0, 1)
                found = out[piece, 0]
                out[piece, found + 1] = (source * slots + slot) * 65536 + row * 256 + col % per_quarter
                out[piece, 0] = found + jnp.where(quarter % 2 == core, 1, 0)
                return carry

            lax.fori_loop(0, codes[offsets * slots + offset], visit, 0)


def weights_kernel(codes, targets, out, sums):
    step = pl.program_id(0)
    slots, side = targets.shape[1], targets.shape[-1]
    blocks = out.shape[0]

    @pl.when(step == 0)
    def _():
        sums[...] = jnp.zeros_like(sums)

    def visit(slot, carry):
        row = codes[step * slots + slot] // 256
        share = 16.0 / targets[0, slot].astype(jnp.float32)
        sums[row] += share * share
        return carry

    lax.fori_loop(0, codes[pl.num_programs(0) * slots + step], visit, 0)

    @pl.when(step == pl.num_programs(0) - 1)
    def _():
        ones = jnp.ones((8, side), jnp.float32)
        for block in range(blocks):
            out[block : block + 1, :] = lax.dot_general(
                ones,
                sums[block],
                (((1,), (1,)), ((), ())),
                precision=lax.Precision.HIGHEST,
                preferred_element_type=jnp.float32,
            )[0:1]


def rows_kernel(place, q0, q1, q2, q3, out):
    side = out.shape[1]
    count = q0.shape[0] // side
    for index, quarter in enumerate((q0, q1, q2, q3)):
        holder = jnp.bitwise_xor(place[0], index)

        def visit(block, carry, quarter=quarter, holder=holder):
            points = quarter[pl.ds(pl.multiple_of(block * side, side), side), :].astype(jnp.float32)
            out[holder * count + block, :, :side] = (-2.0 * points).astype(jnp.bfloat16)
            out[holder * count + block, :, side:] = norm_columns(points, 1.0, 0)
            return carry

        lax.fori_loop(0, count, visit, 0)


def stage_kernel(piece, first, lists, rows, points_ref, own, other, *rest):
    if first:
        acc, right, ring, sems = rest
    else:
        _, acc, right, ring, sems = rest
    side = rows.shape[1]
    slots = own.shape[1]
    offset = piece // 2
    dummy = acc.shape[0] - 1
    total = lists[piece, 0]
    groups = (total + GROUP - 1) // GROUP

    def entry(index):
        return lists[piece, 1 + jnp.minimum(index, total - 1)]

    def fetch(group, slot):
        for unit in range(GROUP):
            tile = entry(group * GROUP + unit) // 65536

            @pl.when(tile < slots)
            def _():
                pltpu.make_async_copy(own.at[offset, tile], ring.at[slot, unit], sems.at[slot, unit]).start()

            @pl.when(tile >= slots)
            def _():
                pltpu.make_async_copy(other.at[offset, tile - slots], ring.at[slot, unit], sems.at[slot, unit]).start()

    @pl.when(groups > 0)
    def _():
        fetch(0, 0)

    if first:
        acc[...] = jnp.zeros_like(acc)

    def build(block, carry):
        points = points_ref[pl.ds(pl.multiple_of(block * side, side), side), :]
        right[block, :, :side] = points
        right[block, :, side:] = norm_columns(points.astype(jnp.float32), 0.0, 3)
        return carry

    lax.fori_loop(0, right.shape[0], build, 0)

    def visit(group, carry):
        slot = lax.rem(group, 2)

        @pl.when(group + 1 < groups)
        def _():
            fetch(group + 1, 1 - slot)

        for unit in range(GROUP):
            pltpu.make_async_copy(own.at[offset, 0], ring.at[slot, unit], sems.at[slot, unit]).wait()
        for unit in range(GROUP):
            index = group * GROUP + unit
            code = entry(index)
            row, col = (code // 256) % 256, code % 256
            right_block = right[col]
            square = lax.dot_general(
                rows[row], right_block, (((1,), (1,)), ((), ())), preferred_element_type=jnp.float32
            )
            share = 1.0 / ring[slot, unit].astype(jnp.float32)
            ratio = (share * (share - lax.rsqrt(square))).astype(jnp.bfloat16)
            place = jnp.where(index < total, row, dummy)
            acc[place] += jnp.dot(ratio, right_block, preferred_element_type=jnp.float32)
        return carry

    lax.fori_loop(0, groups, visit, 0)


def pack_core_kernel(place, acc, weights, for_far, for_near):
    side = acc.shape[1]
    count = (acc.shape[0] - 1) // 4
    for flip, out in ((3, for_far), (1, for_near)):
        base = jnp.bitwise_xor(place[0], flip) * count
        for block in range(count):
            out[block * side : (block + 1) * side, :] = acc[base + block, :, :side]
            out[count * side + block : count * side + block + 1, :] = row_vector(acc[base + block, :, side:])
        out[count * (side + 1) :, :] = weights[pl.ds(pl.multiple_of(base, count), count), :]


def pack_far_kernel(place, acc, weights, got, points_ref, out):
    side = acc.shape[1]
    count = (acc.shape[0] - 1) // 4
    base = jnp.bitwise_xor(place[0], 2) * count
    total_weights = weights[pl.ds(pl.multiple_of(base, count), count), :] + got[count * (side + 1) :, :]
    ratios = []
    for block in range(count):
        rows = slice(block * side, (block + 1) * side)
        points = points_ref[rows, :].astype(jnp.float32)
        pulled = acc[base + block, :, :side] + got[rows, :]
        along = jnp.sum(pulled * points, axis=-1, keepdims=True)
        length = jnp.sum(points * points, axis=-1, keepdims=True)
        share = (along / (length + 1e-6)).astype(jnp.bfloat16).astype(jnp.float32)
        out[rows, :] = (pulled - share * points).astype(jnp.bfloat16)
        ratio = row_vector(acc[base + block, :, side:] - jnp.broadcast_to(share, (side, side)))
        ratios.append(ratio + got[count * side + block : count * side + block + 1, :])
    ratio_rows = jnp.concatenate(ratios, axis=0)
    at = count * side
    for value in (ratio_rows, total_weights):
        for part in split_three(value):
            out[at : at + count, :] = part
            at += count


def finish_kernel(place, acc, weights, near, far, points_ref, out):
    side = acc.shape[1]
    count = (acc.shape[0] - 1) // 4
    base = place[0] * count

    def joined(at):
        parts = [far[at + part * count : at + (part + 1) * count, :].astype(jnp.float32) for part in range(3)]
        return parts[0] + parts[1] + parts[2]

    at = count * side
    ratio_rows = near[at : at + count, :] + joined(at)
    weight_rows = near[at + count : at + 2 * count, :] + joined(at + 3 * count)
    weight_rows = weight_rows + weights[pl.ds(pl.multiple_of(base, count), count), :]
    for block in range(count):
        rows = slice(block * side, (block + 1) * side)
        points = points_ref[rows, :].astype(jnp.float32)
        pulled = acc[base + block, :, :side] + near[rows, :] + far[rows, :].astype(jnp.float32)
        ratio = acc[base + block, :, side : side + 1] + column_vector(ratio_rows[block : block + 1, :], side)
        weight = column_vector(weight_rows[block : block + 1, :], side) + 256.0
        out[rows, :] = points - 256.0 * (ratio * points - pulled) / weight


def moved(value, place):
    cols, reps = lax.axis_size("col"), lax.axis_size("rep")
    pairs = []
    for col in range(cols):
        for rep in range(reps):
            to_col, to_rep = place(col, rep)
            pairs.append((col * reps + rep, (to_col % cols) * reps + to_rep))
    return lax.ppermute(value, ("col", "rep"), pairs)


def per_device(coords, dissim, tile_blocks, tile_count):
    own_rows, width = coords.shape
    _, offsets, slots, side, _ = dissim.shape
    dissim = dissim[0]
    reps = lax.axis_size("rep")
    stride = lax.axis_size("col") // 8
    count = own_rows // side
    blocks = reps * count
    rep = lax.axis_index("rep")
    even = (lax.axis_index("col") // stride) % 2 == 0
    place = jnp.stack([rep, jnp.int32(count)]).astype(jnp.int32)

    def along_y(value):
        return moved(value, lambda col, r: (col, r ^ 2))

    def along_core(value):
        return moved(value, lambda col, r: (col, r ^ 1))

    def along_z(value):
        return moved(value, lambda col, r: (col + 2 * stride, r))

    def along_x(value):
        return moved(value, lambda col, r: (col + stride if (col // stride) % 2 == 0 else col - stride, r))

    def swapped(at_even, at_odd):
        return along_x(jnp.where(even, at_even, at_odd))

    vmem = pl.BlockSpec(memory_space=VMEM)
    smem = pl.BlockSpec(memory_space=SMEM)
    hbm = pl.BlockSpec(memory_space=HBM)

    codes = jnp.concatenate(
        [(tile_blocks[0, :, :, 0] * 256 + tile_blocks[0, :, :, 1]).reshape(-1), tile_count[0]]
    )
    other_codes = along_core(codes)
    other_dissim = along_core(dissim)

    piece = {(0, 0): coords}
    piece[0, 1] = along_y(coords)
    piece[2, 0] = along_z(coords)
    near_rows = along_core(coords)
    far_rows = along_core(piece[0, 1])
    piece[1, 0] = swapped(coords, piece[2, 0])
    piece[2, 1] = along_y(piece[2, 0])
    piece[4, 0] = along_z(piece[2, 0])
    piece[3, 0] = along_z(piece[1, 0])
    piece[1, 1] = swapped(piece[0, 1], piece[2, 1])
    piece[4, 1] = along_y(piece[4, 0])
    piece[3, 1] = swapped(piece[2, 1], piece[4, 1])

    weights = pl.pallas_call(
        weights_kernel,
        out_shape=jax.ShapeDtypeStruct((blocks, side), jnp.float32),
        grid=(offsets,),
        in_specs=[smem, pl.BlockSpec((1, slots, side, side), lambda k: (k, 0, 0, 0))],
        out_specs=vmem,
        scratch_shapes=[VMEM((blocks, side, side), jnp.float32)],
        compiler_params=PARAMS,
        name="row_weights",
    )(codes, dissim)
    lists = pl.pallas_call(
        functools.partial(lists_kernel, slots),
        out_shape=jax.ShapeDtypeStruct((2 * offsets, 2 * slots + 2), jnp.int32),
        in_specs=[smem] * 3,
        out_specs=smem,
        name="sort_slots",
    )(place, codes, other_codes)
    rows = pl.pallas_call(
        rows_kernel,
        out_shape=VMEM((blocks, side, 2 * side), jnp.bfloat16),
        in_specs=[smem] + [vmem] * 4,
        out_specs=vmem,
        compiler_params=PARAMS,
        name="row_operands",
    )(place, coords, near_rows, piece[0, 1], far_rows)

    acc = None
    for key in ((0, 0), (0, 1), (2, 0), (1, 0), (2, 1), (4, 0), (3, 0), (1, 1), (4, 1), (3, 1)):
        first = acc is None
        acc = pl.pallas_call(
            functools.partial(stage_kernel, 2 * key[0] + key[1], first),
            out_shape=VMEM((blocks + 1, side, 2 * side), jnp.float32),
            in_specs=[smem, vmem, vmem, hbm, hbm] + ([] if first else [vmem]),
            out_specs=vmem,
            input_output_aliases={} if first else {5: 0},
            scratch_shapes=[
                VMEM((count, side, 2 * side), jnp.bfloat16),
                VMEM((2, GROUP, side, side), jnp.bfloat16),
                pltpu.SemaphoreType.DMA((2, GROUP)),
            ],
            compiler_params=PARAMS,
            name=f"tiles_{key[0]}_{key[1]}",
        )(lists, rows, piece[key], dissim, other_dissim, *([] if first else [acc]))

    message = jax.ShapeDtypeStruct((own_rows + 2 * count, side), jnp.float32)
    for_far, for_near = pl.pallas_call(
        pack_core_kernel,
        out_shape=(message, message),
        in_specs=[smem, vmem, vmem],
        out_specs=(vmem, vmem),
        compiler_params=PARAMS,
        name="pack_core",
    )(place, acc, weights)
    got_far = along_core(for_far)
    got_near = along_core(for_near)
    to_far = pl.pallas_call(
        pack_far_kernel,
        out_shape=jax.ShapeDtypeStruct((own_rows + 6 * count, side), jnp.bfloat16),
        in_specs=[smem] + [vmem] * 4,
        out_specs=vmem,
        compiler_params=PARAMS,
        name="pack_far",
    )(place, acc, weights, got_far, piece[0, 1])
    far = along_y(to_far)
    return pl.pallas_call(
        finish_kernel,
        out_shape=jax.ShapeDtypeStruct((own_rows, width), jnp.float32),
        in_specs=[smem] + [vmem] * 5,
        out_specs=vmem,
        compiler_params=PARAMS,
        name="finish",
    )(place, acc, weights, got_near, far, coords)


def solution(mesh):
    in_specs = (
        P(("col", "rep"), None),
        P(("col", "rep"), None, None, None, None),
        P(("col", "rep"), None, None, None),
        P(("col", "rep"), None),
    )
    out_specs = P(("col", "rep"), None)
    return jax.shard_map(
        per_device, mesh=mesh, in_specs=in_specs, out_specs=out_specs, check_vma=False
    )
```

```python
import functools

import jax
import jax.numpy as jnp
from jax import lax
from jax.experimental import pallas as pl
from jax.experimental.pallas import tpu as pltpu
from jax.sharding import PartitionSpec as P

GROUP = 16
SUM_GROUP = 8
COST = 0.25
VMEM, SMEM, HBM = pltpu.VMEM, pltpu.SMEM, pltpu.HBM
STAGES = (
    ((0, 0), (1, 1), (4, 4)),
    ((-1, 2), (2, 6), (5, 5), (8, 8)),
    ((9, 9), (3, 7), (6, 3)),
    ((7, -1),),
)


def lanes_of(shape):
    return lax.broadcasted_iota(jnp.int32, shape, len(shape) - 1)


def diagonal(side):
    return lax.broadcasted_iota(jnp.int32, (side, side), 0) == lanes_of((side, side))


def row_of(column):
    return jnp.sum(jnp.where(diagonal(column.shape[0]), column, 0.0), axis=0, keepdims=True)


def column_of(row):
    return jnp.sum(jnp.where(diagonal(row.shape[1]), row, 0.0), axis=1, keepdims=True)


def lists_kernel(per_quarter, place, codes, out):
    core, mine, even = place[0] % 2, place[0] // 2, place[1] == 1
    offsets, width = codes.shape
    room = out.shape[1] - 128
    lanes = lanes_of((1, width))
    later = lax.broadcasted_iota(jnp.int32, (width, width), 0) <= lanes_of((width, width))
    later = jnp.where(later, 1.0, 0.0).astype(jnp.bfloat16)
    place_of = lax.broadcasted_iota(jnp.int32, (room, width), 0).astype(jnp.float32) + 1.0
    for stage, arrays in enumerate(STAGES):
        before = jnp.zeros((1, 1), jnp.float32)
        listed = jnp.zeros((32, room), jnp.float32)
        for offset in range(offsets):
            here = [(m, *pair) for m, pair in enumerate(arrays) if offset in (pair[0] // 2, pair[1] // 2)]
            if not here:
                continue
            code = codes[offset : offset + 1, :]
            row, col = lax.shift_right_arithmetic(code, 8), code & 255
            quarter = jnp.zeros_like(col)
            for edge in range(1, 4):
                quarter += jnp.where(col >= edge * per_quarter, 1, 0)
            match = jnp.zeros((1, width), jnp.float32)
            column = (col - quarter * per_quarter).astype(jnp.float32)
            for index, at_even, at_odd in here:
                piece = jnp.where(even, at_even, at_odd)
                wanted = jnp.bitwise_xor(mine, piece & 1) * 2 + core
                wanted = jnp.where(lax.shift_right_arithmetic(piece, 1) == offset, wanted, -1)
                hit = jnp.where((code >= 0) & (quarter == wanted), 1.0, 0.0)
                match += hit
                column += hit * (index * per_quarter)
            found = before + jnp.dot(
                jnp.broadcast_to(match, (16, width)).astype(jnp.bfloat16), later, preferred_element_type=jnp.float32
            )[0:1]
            before += jnp.sum(match, axis=1, keepdims=True)
            chosen = jnp.where((place_of == found) & (match > 0.0), 1.0, 0.0).astype(jnp.bfloat16)
            values = [lanes.astype(jnp.float32), row.astype(jnp.float32), column, jnp.full((1, width), offset, jnp.float32)]
            values = jnp.concatenate([jnp.broadcast_to(v, (8, width)) for v in values], axis=0).astype(jnp.bfloat16)
            listed += lax.dot_general(
                values, chosen, (((1,), (1,)), ((), ())), preferred_element_type=jnp.float32
            )
        listed = listed.astype(jnp.int32)
        lane, row, column, offset = listed[0:1], listed[8:9], listed[16:17], listed[24:25]
        slots = width // 2
        tile = offset * slots + lane + jnp.where(lane >= slots, (offsets - 1) * slots, 0)
        out[stage : stage + 1, :room] = tile * 65536 + row * 256 + column
        out[stage : stage + 1, room:] = jnp.broadcast_to(before.astype(jnp.int32), (1, 128))


def weights_kernel(codes, counts, targets, out, sums):
    step = pl.program_id(0)
    blocks, side = out.shape
    total = counts[step]

    @pl.when(step == 0)
    def _():
        sums[...] = jnp.zeros_like(sums)

    def visit(group, carry):
        for unit in range(SUM_GROUP):
            slot = group * SUM_GROUP + unit
            row = jnp.where(slot < total, lax.shift_right_arithmetic(codes[step, slot], 8), blocks)
            share = pltpu.reciprocal(targets[0, slot].astype(jnp.float32), approx=True)
            sums[row] += share * share
        return carry

    lax.fori_loop(0, (total + SUM_GROUP - 1) // SUM_GROUP, visit, 0)

    @pl.when(step == pl.num_programs(0) - 1)
    def _():
        def close(group, carry):
            for unit in range(8):
                whole = jnp.sum(sums[group * 8 + unit], axis=1, keepdims=True)
                out[pl.ds(group * 8 + unit, 1), :] = row_of(whole)
            return carry

        lax.fori_loop(0, blocks // 8, close, 0)


def scale_kernel(place, weights, out):
    count = weights.shape[0] // 4
    side = weights.shape[1]
    own = weights[pl.ds(pl.multiple_of(place[0] * count, count), count), :]
    for block in range(count):
        total = column_of(own[block : block + 1, :])
        out[block * side : (block + 1) * side, :] = jnp.broadcast_to(1.0 / (total + 1.0), (side, side))


def rows_kernel(place, q0, q1, q2, q3, out, norms):
    side = out.shape[1]
    count = q0.shape[0] // side
    for index, quarter in enumerate((q0, q1, q2, q3)):
        holder = jnp.bitwise_xor(place[0], index)

        def visit(block, carry, quarter=quarter, holder=holder):
            points = quarter[pl.ds(pl.multiple_of(block * side, side), side), :].astype(jnp.float32)
            out[holder * count + block] = (-2.0 * points).astype(jnp.bfloat16)
            norm = jnp.sum(points * points, axis=1, keepdims=True) + 1.0
            norms[holder * count + block] = jnp.broadcast_to(norm, (side, side))
            return carry

        lax.fori_loop(0, count, visit, 0, unroll=4)


def stage_kernel(stage, first, parts, lists, rows, norms, *rest):
    points_refs, (own, other), rest = rest[:parts], rest[parts : parts + 2], rest[parts + 2 :]
    if not first:
        rest = rest[2:]
    pulled, summed, token, right, column_norms, ring, ratios, sems = rest
    side = rows.shape[1]
    tiles = own.shape[0]
    dummy = pulled.shape[0] - 1
    total = lists[stage, lists.shape[1] - 1]
    groups = (total + GROUP - 1) // GROUP
    token[...] = jnp.zeros_like(token)

    def entry(index):
        return lists[stage, jnp.minimum(index, total - 1)]

    def fetch(group, slot):
        for unit in range(GROUP):
            tile = lax.shift_right_arithmetic(entry(group * GROUP + unit), 16)

            @pl.when(tile < tiles)
            def _():
                pltpu.make_async_copy(own.at[tile], ring.at[slot, unit], sems.at[slot]).start()

            @pl.when(tile >= tiles)
            def _():
                pltpu.make_async_copy(other.at[tile - tiles], ring.at[slot, unit], sems.at[slot]).start()

    @pl.when(groups > 0)
    def _():
        fetch(0, 0)

    if first:
        pulled[...] = jnp.zeros_like(pulled)
        summed[...] = jnp.zeros_like(summed)

    @pl.when(groups > 0)
    def _():
        at = 0
        for points_ref in points_refs:
            held = points_ref.shape[0] // side

            def build(block, carry, points_ref=points_ref, at=at):
                points = points_ref[pl.ds(pl.multiple_of(block * side, side), side), :]
                right[at + block] = points
                points = points.astype(jnp.float32)
                column_norms[pl.ds(at + block, 1), :] = row_of(jnp.sum(points * points, axis=1, keepdims=True))
                return carry

            lax.fori_loop(0, held, build, 0, unroll=4)
            at += held

    def visit(group, carry):
        slot = lax.rem(group, 2)

        @pl.when(group + 1 < groups)
        def _():
            fetch(group + 1, 1 - slot)

        pltpu.make_async_copy(own.at[pl.ds(0, GROUP)], ring.at[slot], sems.at[slot]).wait()
        for unit in range(GROUP):
            code = entry(group * GROUP + unit)
            row, column = lax.shift_right_arithmetic(code, 8) & 255, code & 255
            square = lax.dot_general(
                rows[row], right[column], (((1,), (1,)), ((), ())), preferred_element_type=jnp.float32
            )
            square += norms[row] + column_norms[pl.ds(column, 1), :]
            share = pltpu.reciprocal(ring[slot, unit].astype(jnp.float32), approx=True)
            ratios[unit] = (share * (share - lax.rsqrt(square))).astype(jnp.bfloat16)
        for unit in range(GROUP):
            index = group * GROUP + unit
            code = entry(index)
            place = jnp.where(index < total, lax.shift_right_arithmetic(code, 8) & 255, dummy)
            pulled[place] += jnp.dot(ratios[unit], right[code & 255], preferred_element_type=jnp.float32)
            summed[place] += ratios[unit].astype(jnp.float32)
        return carry

    lax.fori_loop(0, groups, visit, 0)


def gate_kernel(*refs):
    pass


def drift(pulled, summed, block, points):
    return pulled[block] - jnp.sum(summed[block], axis=1, keepdims=True) * points


def pack_core_kernel(flip, place, pulled, summed, points_ref, out):
    side = pulled.shape[1]
    count = (pulled.shape[0] - 1) // 4
    base = jnp.bitwise_xor(place[0], flip) * count
    for block in range(count):
        rows = slice(block * side, (block + 1) * side)
        out[rows, :] = drift(pulled, summed, base + block, points_ref[rows, :].astype(jnp.float32))


def pack_far_kernel(place, pulled, summed, got, points_ref, out):
    side = pulled.shape[1]
    count = (pulled.shape[0] - 1) // 4
    base = jnp.bitwise_xor(place[0], 2) * count
    shares = []
    for block in range(count):
        rows = slice(block * side, (block + 1) * side)
        points = points_ref[rows, :].astype(jnp.float32)
        total = drift(pulled, summed, base + block, points) + got[rows, :]
        along = jnp.sum(total * points, axis=-1, keepdims=True)
        length = jnp.sum(points * points, axis=-1, keepdims=True)
        share = (along / (length + 1e-6)).astype(jnp.bfloat16).astype(jnp.float32)
        out[rows, :] = (total - share * points).astype(jnp.bfloat16)
        shares.append(row_of(share))
    out[count * side :, :] = jnp.concatenate(shares, axis=0).astype(jnp.bfloat16)


def finish_kernel(place, pulled, summed, near, far, scale, points_ref, out):
    side = pulled.shape[1]
    count = (pulled.shape[0] - 1) // 4
    base = place[0] * count
    shares = far[count * side :, :].astype(jnp.float32)
    for block in range(count):
        rows = slice(block * side, (block + 1) * side)
        points = points_ref[rows, :].astype(jnp.float32)
        total = drift(pulled, summed, base + block, points) + near[rows, :] + far[rows, :].astype(jnp.float32)
        total = total + column_of(shares[block : block + 1, :]) * points
        out[rows, :] = points + scale[rows, :] * total


def kernel_call(body, name, cost, **options):
    return pl.pallas_call(
        body,
        name=name,
        compiler_params=pltpu.CompilerParams(vmem_limit_bytes=40 * 1024 * 1024),
        cost_estimate=pl.CostEstimate(
            flops=int(cost * COST * 1e9), bytes_accessed=int(cost * COST * 3e6), transcendentals=0
        ),
        **options,
    )


def per_device(coords, dissim, tile_blocks, tile_count):
    own_rows, width = coords.shape
    _, offsets, slots, side, _ = dissim.shape
    targets = dissim.reshape(offsets * slots, side, side)
    reps = lax.axis_size("rep")
    stride = lax.axis_size("col") // 8
    count = own_rows // side
    blocks = reps * count
    rep = lax.axis_index("rep")
    even = (lax.axis_index("col") // stride) % 2 == 0
    place = jnp.stack([rep, even.astype(jnp.int32)])

    def sent(value, place, parity=None):
        cols = lax.axis_size("col")
        pairs = []
        for col in range(cols):
            if parity is None or (col // stride) % 2 == parity:
                for r in range(reps):
                    to_col, to_rep = place(col, r)
                    pairs.append((col * reps + r, (to_col % cols) * reps + to_rep))
        return lax.ppermute(value, ("col", "rep"), pairs)

    def along_y(value, parity=None):
        return sent(value, lambda col, r: (col, r ^ 2), parity)

    def along_core(value):
        return sent(value, lambda col, r: (col, r ^ 1))

    def along_z(value, parity=None):
        return sent(value, lambda col, r: (col + 2 * stride, r), parity)

    def along_x(value, parity=None):
        return sent(value, lambda col, r: (col + stride if (col // stride) % 2 == 0 else col - stride, r), parity)

    vmem = pl.BlockSpec(memory_space=VMEM)
    smem = pl.BlockSpec(memory_space=SMEM)
    hbm = pl.BlockSpec(memory_space=HBM)
    anywhere = pl.BlockSpec(memory_space=pl.ANY)

    codes = tile_blocks[0, :, :, 0] * 256 + tile_blocks[0, :, :, 1]
    alive = jnp.arange(slots, dtype=jnp.int32)[None, :] < tile_count[0][:, None]
    codes = jnp.where(alive, codes, -1)
    other_codes = along_core(codes)
    other_targets = along_core(targets)

    def gated(values, tokens):
        return kernel_call(
            gate_kernel,
            "gate",
            0.3,
            out_shape=tuple(jax.ShapeDtypeStruct(v.shape, v.dtype) for v in values),
            in_specs=[anywhere] * (len(values) + len(tokens)),
            out_specs=(anywhere,) * len(values),
            input_output_aliases={i: i for i in range(len(values))},
        )(*values, *tokens)

    weights = kernel_call(
        weights_kernel,
        "row_weights",
        9,
        out_shape=jax.ShapeDtypeStruct((blocks, side), jnp.float32),
        grid=(offsets,),
        in_specs=[smem, smem, pl.BlockSpec((1, slots, side, side), lambda k: (k, 0, 0, 0))],
        out_specs=vmem,
        scratch_shapes=[VMEM((blocks + 1, side, side), jnp.float32)],
    )(codes, tile_count[0], pltpu.with_memory_space_constraint(dissim[0], HBM))
    lists = kernel_call(
        functools.partial(lists_kernel, count),
        "sort_slots",
        2,
        out_shape=jax.ShapeDtypeStruct((len(STAGES), 2 * slots * (offsets - 1) + 128), jnp.int32),
        in_specs=[smem, vmem],
        out_specs=vmem,
    )(place, jnp.concatenate([codes, other_codes], axis=1))
    p01 = along_y(coords)
    p20 = along_z(coords)
    a10 = along_x(coords, 0)
    near_rows = along_core(coords)
    p20, p01, weights = gated((p20, p01, weights), ())
    far_rows = along_core(p01)
    p40 = along_z(p20)
    p21 = along_y(p20)
    s20 = along_x(p20)
    b11 = along_x(p01, 0)
    weights = weights + along_core(weights)
    rows, norms = kernel_call(
        rows_kernel,
        "row_operands",
        3,
        out_shape=(VMEM((blocks, side, side), jnp.bfloat16), VMEM((blocks, side, side), jnp.float32)),
        in_specs=[smem] + [vmem] * 4,
        out_specs=(vmem, vmem),
    )(place, coords, near_rows, p01, far_rows)

    def tiles(stage, sums, *points):
        first = sums is None
        held = sum(p.shape[0] for p in points) // side
        sums_shape = VMEM((blocks + 1, side, side), jnp.float32)
        out = kernel_call(
            functools.partial(stage_kernel, stage, first, len(points)),
            f"tiles_{stage}",
            1 + 2.0 * len(STAGES[stage]),
            out_shape=(sums_shape, sums_shape, jax.ShapeDtypeStruct((8, side), jnp.float32)),
            in_specs=[smem, vmem, vmem] + [vmem] * len(points) + [hbm, hbm] + ([] if first else [vmem, vmem]),
            out_specs=(vmem, vmem, vmem),
            input_output_aliases={} if first else {5 + len(points): 0, 6 + len(points): 1},
            scratch_shapes=[
                VMEM((held, side, side), jnp.bfloat16),
                VMEM((held, side), jnp.float32),
                VMEM((2, GROUP, side, side), jnp.bfloat16),
                VMEM((GROUP, side, side), jnp.bfloat16),
                pltpu.SemaphoreType.DMA((2,)),
            ],
        )(lists, rows, pltpu.with_memory_space_constraint(norms, VMEM), *points, targets, other_targets, *([] if first else sums))
        return out[:2], out[2]

    sums, token = tiles(0, None, coords, p01, p20)
    p40, p21, s20, weights = gated((p40, p21, s20, weights), (token,))
    p41 = along_y(p40)
    t21 = along_x(p21)
    c30 = along_z(s20, 0)
    weights = weights + along_y(weights)
    sums, token = tiles(1, sums, a10, s20, p21, p40)
    p41, t21, weights = gated((p41, t21, weights), (token,))
    half = own_rows // 2
    d31 = along_x(p41[:half], 1), along_z(t21[half:], 0)
    scale = kernel_call(
        scale_kernel,
        "row_scale",
        1,
        out_shape=jax.ShapeDtypeStruct((own_rows, side), jnp.float32),
        in_specs=[smem, vmem],
        out_specs=vmem,
    )(place, weights)
    sums, token = tiles(2, sums, p41, t21, jnp.where(even, c30, b11))
    sums, token = tiles(3, sums, *d31)

    def pack_core(flip, name, points):
        return kernel_call(
            functools.partial(pack_core_kernel, flip),
            name,
            1,
            out_shape=jax.ShapeDtypeStruct((own_rows, side), jnp.float32),
            in_specs=[smem] + [vmem] * 3,
            out_specs=vmem,
        )(place, *sums, points)

    got_far = along_core(pack_core(3, "pack_core_far", far_rows))
    to_far = kernel_call(
        pack_far_kernel,
        "pack_far",
        1.5,
        out_shape=jax.ShapeDtypeStruct((own_rows + count, side), jnp.bfloat16),
        in_specs=[smem] + [vmem] * 4,
        out_specs=vmem,
    )(place, *sums, got_far, p01)
    far = along_y(to_far)
    got_near = along_core(pack_core(1, "pack_core_near", near_rows))
    return kernel_call(
        finish_kernel,
        "finish",
        1.5,
        out_shape=jax.ShapeDtypeStruct((own_rows, width), jnp.float32),
        in_specs=[smem] + [vmem] * 6,
        out_specs=vmem,
    )(place, *sums, got_near, far, scale, coords)


def solution(mesh):
    in_specs = (
        P(("col", "rep"), None),
        P(("col", "rep"), None, None, None, None),
        P(("col", "rep"), None, None, None),
        P(("col", "rep"), None),
    )
    out_specs = P(("col", "rep"), None)
    return jax.shard_map(
        per_device, mesh=mesh, in_specs=in_specs, out_specs=out_specs, check_vma=False
    )
```

```python
import functools

import jax
import jax.numpy as jnp
from jax import lax
from jax.experimental import pallas as pl
from jax.experimental.pallas import tpu as pltpu
from jax.sharding import PartitionSpec as P

GROUP = 16
SUM_GROUP = 8
COST = 0.25
VMEM_LIMIT = 40 * 1024 * 1024
VMEM, SMEM, HBM = pltpu.VMEM, pltpu.SMEM, pltpu.HBM
STAGES = (
    ((0, 0), (1, 1), (4, 4)),
    ((2, 2), (5, 5), (8, 8)),
    ((9, 9), (3, 7), (6, 6)),
    ((7, 3),),
)


def lanes_of(shape):
    return lax.broadcasted_iota(jnp.int32, shape, len(shape) - 1)


def diagonal(side):
    return lax.broadcasted_iota(jnp.int32, (side, side), 0) == lanes_of((side, side))


def row_of(column):
    return jnp.sum(jnp.where(diagonal(column.shape[0]), column, 0.0), axis=0, keepdims=True)


def column_of(row):
    return jnp.sum(jnp.where(diagonal(row.shape[1]), row, 0.0), axis=1, keepdims=True)


def lists_kernel(per_quarter, place, codes, out):
    core, mine, even = place[0] % 2, place[0] // 2, place[1] == 1
    offsets, width = codes.shape
    room = out.shape[1] - 128
    lanes = lanes_of((1, width))
    later = lax.broadcasted_iota(jnp.int32, (width, width), 0) <= lanes_of((width, width))
    later = jnp.where(later, 1.0, 0.0).astype(jnp.bfloat16)
    place_of = lax.broadcasted_iota(jnp.int32, (room, width), 0).astype(jnp.float32) + 1.0
    for stage, arrays in enumerate(STAGES):
        before = jnp.zeros((1, 1), jnp.float32)
        listed = jnp.zeros((32, room), jnp.float32)
        for offset in range(offsets):
            here = [(m, *pair) for m, pair in enumerate(arrays) if offset in (pair[0] // 2, pair[1] // 2)]
            if not here:
                continue
            code = codes[offset : offset + 1, :]
            row, col = lax.shift_right_arithmetic(code, 8), code & 255
            quarter = jnp.zeros_like(col)
            for edge in range(1, 4):
                quarter += jnp.where(col >= edge * per_quarter, 1, 0)
            match = jnp.zeros((1, width), jnp.float32)
            column = (col - quarter * per_quarter).astype(jnp.float32)
            for index, at_even, at_odd in here:
                piece = jnp.where(even, at_even, at_odd)
                wanted = jnp.bitwise_xor(mine, piece & 1) * 2 + core
                wanted = jnp.where(lax.shift_right_arithmetic(piece, 1) == offset, wanted, -1)
                hit = jnp.where((code >= 0) & (quarter == wanted), 1.0, 0.0)
                match += hit
                column += hit * (index * per_quarter)
            found = before + jnp.dot(
                jnp.broadcast_to(match, (16, width)).astype(jnp.bfloat16), later, preferred_element_type=jnp.float32
            )[0:1]
            before += jnp.sum(match, axis=1, keepdims=True)
            chosen = jnp.where((place_of == found) & (match > 0.0), 1.0, 0.0).astype(jnp.bfloat16)
            values = [lanes.astype(jnp.float32), row.astype(jnp.float32), column, jnp.full((1, width), offset, jnp.float32)]
            values = jnp.concatenate([jnp.broadcast_to(v, (8, width)) for v in values], axis=0).astype(jnp.bfloat16)
            listed += lax.dot_general(
                values, chosen, (((1,), (1,)), ((), ())), preferred_element_type=jnp.float32
            )
        listed = listed.astype(jnp.int32)
        lane, row, column, offset = listed[0:1], listed[8:9], listed[16:17], listed[24:25]
        slots = width // 2
        tile = offset * slots + lane + jnp.where(lane >= slots, (offsets - 1) * slots, 0)
        out[stage : stage + 1, :room] = tile * 65536 + row * 256 + column
        out[stage : stage + 1, room:] = jnp.broadcast_to(before.astype(jnp.int32), (1, 128))


def weights_kernel(codes, counts, targets, out, sums):
    step = pl.program_id(0)
    blocks, side = out.shape
    total = counts[step]

    @pl.when(step == 0)
    def _():
        sums[...] = jnp.zeros_like(sums)

    def visit(group, carry):
        for unit in range(SUM_GROUP):
            slot = group * SUM_GROUP + unit
            row = jnp.where(slot < total, lax.shift_right_arithmetic(codes[step, slot], 8), blocks)
            share = pltpu.reciprocal(targets[0, slot].astype(jnp.float32), approx=True)
            sums[row] += share * share
        return carry

    lax.fori_loop(0, (total + SUM_GROUP - 1) // SUM_GROUP, visit, 0)

    @pl.when(step == pl.num_programs(0) - 1)
    def _():
        def close(group, carry):
            for unit in range(8):
                whole = jnp.sum(sums[group * 8 + unit], axis=1, keepdims=True)
                out[pl.ds(group * 8 + unit, 1), :] = row_of(whole)
            return carry

        lax.fori_loop(0, blocks // 8, close, 0)


def scale_kernel(place, weights, out):
    count = weights.shape[0] // 4
    side = weights.shape[1]
    own = weights[pl.ds(pl.multiple_of(place[0] * count, count), count), :]
    for block in range(count):
        total = column_of(own[block : block + 1, :])
        out[block * side : (block + 1) * side, :] = jnp.broadcast_to(1.0 / (total + 1.0), (side, side))


def rows_kernel(place, q0, q1, q2, q3, out, norms):
    side = out.shape[1]
    count = q0.shape[0] // side
    for index, quarter in enumerate((q0, q1, q2, q3)):
        holder = jnp.bitwise_xor(place[0], index)

        def visit(block, carry, quarter=quarter, holder=holder):
            points = quarter[pl.ds(pl.multiple_of(block * side, side), side), :].astype(jnp.float32)
            out[holder * count + block] = (-2.0 * points).astype(jnp.bfloat16)
            norm = jnp.sum(points * points, axis=1, keepdims=True) + 1.0
            norms[holder * count + block] = jnp.broadcast_to(norm, (side, side))
            return carry

        lax.fori_loop(0, count, visit, 0, unroll=4)


def stage_kernel(stage, first, layout, place, lists, rows, norms, *rest):
    parts = len(layout)
    points_refs, (own, other), rest = rest[:parts], rest[parts : parts + 2], rest[parts + 2 :]
    if not first:
        rest = rest[2:]
    pulled, summed, token, right, column_norms, ring, ratios, sems = rest
    side = rows.shape[1]
    tiles = own.shape[0]
    dummy = pulled.shape[0] - 1
    total = lists[stage, lists.shape[1] - 1]
    groups = (total + GROUP - 1) // GROUP
    token[...] = jnp.zeros_like(token)

    def entry(index):
        return lists[stage, jnp.minimum(index, total - 1)]

    def fetch(group, slot):
        for unit in range(GROUP):
            tile = lax.shift_right_arithmetic(entry(group * GROUP + unit), 16)

            @pl.when(tile < tiles)
            def _():
                pltpu.make_async_copy(own.at[tile], ring.at[slot, unit], sems.at[slot]).start()

            @pl.when(tile >= tiles)
            def _():
                pltpu.make_async_copy(other.at[tile - tiles], ring.at[slot, unit], sems.at[slot]).start()

    @pl.when(groups > 0)
    def _():
        fetch(0, 0)

    if first:
        pulled[...] = jnp.zeros_like(pulled)
        summed[...] = jnp.zeros_like(summed)

    @pl.when(groups > 0)
    def _():
        for points_ref, (at, parity) in zip(points_refs, layout, strict=True):

            def build(block, carry, points_ref=points_ref, at=at):
                points = points_ref[pl.ds(pl.multiple_of(block * side, side), side), :]
                right[at + block] = points
                points = points.astype(jnp.float32)
                column_norms[pl.ds(at + block, 1), :] = row_of(jnp.sum(points * points, axis=1, keepdims=True))
                return carry

            held = jnp.where(jnp.bool_(parity is None) | (place[1] == parity), points_ref.shape[0] // side // 4, 0)

            def build_four(four, carry, build=build):
                for unit in range(4):
                    build(four * 4 + unit, carry)
                return carry

            lax.fori_loop(0, held, build_four, 0)

    def visit(group, carry):
        slot = lax.rem(group, 2)

        @pl.when(group + 1 < groups)
        def _():
            fetch(group + 1, 1 - slot)

        pltpu.make_async_copy(own.at[pl.ds(0, GROUP)], ring.at[slot], sems.at[slot]).wait()
        for unit in range(GROUP):
            code = entry(group * GROUP + unit)
            row, column = lax.shift_right_arithmetic(code, 8) & 255, code & 255
            square = lax.dot_general(
                rows[row], right[column], (((1,), (1,)), ((), ())), preferred_element_type=jnp.float32
            )
            square += norms[row] + column_norms[pl.ds(column, 1), :]
            share = pltpu.reciprocal(ring[slot, unit].astype(jnp.float32), approx=True)
            ratios[unit] = (share * (share - lax.rsqrt(square))).astype(jnp.bfloat16)
        for unit in range(GROUP):
            index = group * GROUP + unit
            code = entry(index)
            place = jnp.where(index < total, lax.shift_right_arithmetic(code, 8) & 255, dummy)
            pulled[place] += jnp.dot(ratios[unit], right[code & 255], preferred_element_type=jnp.float32)
            summed[place] += ratios[unit].astype(jnp.float32)
        return carry

    lax.fori_loop(0, groups, visit, 0)


def gate_kernel(*refs):
    pass


def choose_kernel(place, at_even, at_odd, out):
    @pl.when(place[1] == 1)
    def _():
        out[...] = at_even[...]

    @pl.when(place[1] == 0)
    def _():
        out[...] = at_odd[...]


def drift(pulled, summed, block, points):
    return pulled[block] - jnp.sum(summed[block], axis=1, keepdims=True) * points


def pack_core_kernel(flip, place, pulled, summed, points_ref, out):
    side = pulled.shape[1]
    count = (pulled.shape[0] - 1) // 4
    base = jnp.bitwise_xor(place[0], flip) * count
    for block in range(count):
        rows = slice(block * side, (block + 1) * side)
        out[rows, :] = drift(pulled, summed, base + block, points_ref[rows, :].astype(jnp.float32))


def pack_far_kernel(place, pulled, summed, got, points_ref, out):
    side = pulled.shape[1]
    count = (pulled.shape[0] - 1) // 4
    base = jnp.bitwise_xor(place[0], 2) * count
    shares = []
    for block in range(count):
        rows = slice(block * side, (block + 1) * side)
        points = points_ref[rows, :].astype(jnp.float32)
        total = drift(pulled, summed, base + block, points) + got[rows, :]
        along = jnp.sum(total * points, axis=-1, keepdims=True)
        length = jnp.sum(points * points, axis=-1, keepdims=True)
        share = (along / (length + 1e-6)).astype(jnp.bfloat16).astype(jnp.float32)
        out[rows, :] = (total - share * points).astype(jnp.bfloat16)
        shares.append(row_of(share))
    out[count * side :, :] = jnp.concatenate(shares, axis=0).astype(jnp.bfloat16)


def finish_kernel(place, pulled, summed, near, far, scale, points_ref, out):
    side = pulled.shape[1]
    count = (pulled.shape[0] - 1) // 4
    base = place[0] * count
    shares = far[count * side :, :].astype(jnp.float32)
    for block in range(count):
        rows = slice(block * side, (block + 1) * side)
        points = points_ref[rows, :].astype(jnp.float32)
        total = drift(pulled, summed, base + block, points) + near[rows, :] + far[rows, :].astype(jnp.float32)
        total = total + column_of(shares[block : block + 1, :]) * points
        out[rows, :] = points + scale[rows, :] * total


def kernel_call(body, name, cost, **options):
    return pl.pallas_call(
        body,
        name=name,
        compiler_params=pltpu.CompilerParams(vmem_limit_bytes=VMEM_LIMIT),
        cost_estimate=pl.CostEstimate(
            flops=int(cost * COST * 1e9), bytes_accessed=int(cost * COST * 3e6), transcendentals=0
        ),
        **options,
    )


def per_device(coords, dissim, tile_blocks, tile_count):
    own_rows, width = coords.shape
    _, offsets, slots, side, _ = dissim.shape
    targets = dissim.reshape(offsets * slots, side, side)
    reps = lax.axis_size("rep")
    stride = lax.axis_size("col") // 8
    count = own_rows // side
    blocks = reps * count
    rep = lax.axis_index("rep")
    even = (lax.axis_index("col") // stride) % 2 == 0
    place = jnp.stack([rep, even.astype(jnp.int32)])

    def sent(value, place):
        cols = lax.axis_size("col")
        pairs = []
        for col in range(cols):
            for r in range(reps):
                to_col, to_rep = place(col, r)
                pairs.append((col * reps + r, (to_col % cols) * reps + to_rep))
        return lax.ppermute(value, ("col", "rep"), pairs)

    def along_y(value):
        return sent(value, lambda col, r: (col, r ^ 2))

    def along_core(value):
        return sent(value, lambda col, r: (col, r ^ 1))

    def along_z(value):
        return sent(value, lambda col, r: (col + 2 * stride, r))

    def along_x(value):
        return sent(value, lambda col, r: (col + stride if (col // stride) % 2 == 0 else col - stride, r))

    vmem = pl.BlockSpec(memory_space=VMEM)
    smem = pl.BlockSpec(memory_space=SMEM)
    hbm = pl.BlockSpec(memory_space=HBM)
    anywhere = pl.BlockSpec(memory_space=pl.ANY)

    codes = tile_blocks[0, :, :, 0] * 256 + tile_blocks[0, :, :, 1]
    alive = jnp.arange(slots, dtype=jnp.int32)[None, :] < tile_count[0][:, None]
    codes = jnp.where(alive, codes, -1)
    other_codes = along_core(codes)
    other_targets = along_core(targets)

    def gated(values, *tokens):
        return kernel_call(
            gate_kernel,
            "gate",
            0.3,
            out_shape=tuple(jax.ShapeDtypeStruct(v.shape, v.dtype) for v in values),
            in_specs=[anywhere] * (len(values) + len(tokens)),
            out_specs=(anywhere,) * len(values),
            input_output_aliases={i: i for i in range(len(values))},
        )(*values, *tokens)

    weights = kernel_call(
        weights_kernel,
        "row_weights",
        9,
        out_shape=jax.ShapeDtypeStruct((blocks, side), jnp.float32),
        grid=(offsets,),
        in_specs=[smem, smem, pl.BlockSpec((1, slots, side, side), lambda k: (k, 0, 0, 0))],
        out_specs=vmem,
        scratch_shapes=[VMEM((blocks + 1, side, side), jnp.float32)],
    )(codes, tile_count[0], pltpu.with_memory_space_constraint(dissim[0], HBM))
    lists = kernel_call(
        functools.partial(lists_kernel, count),
        "sort_slots",
        2,
        out_shape=jax.ShapeDtypeStruct((len(STAGES), 2 * slots * (offsets - 1) + 128), jnp.int32),
        in_specs=[smem, vmem],
        out_specs=vmem,
    )(place, jnp.concatenate([codes, other_codes], axis=1))
    def chosen(at_even, at_odd):
        return kernel_call(
            choose_kernel,
            "choose",
            0.5,
            out_shape=VMEM(at_even.shape, at_even.dtype),
            in_specs=[smem, vmem, vmem],
            out_specs=vmem,
        )(place, at_even, at_odd)

    def tiles(stage, sums, *places):
        first = sums is None
        points, layout, at = [], [], 0
        for choices in places:
            choices = [(None, choices)] if not isinstance(choices, dict) else list(choices.items())
            for parity, arrays in choices:
                start = at
                for array in arrays:
                    points.append(array)
                    layout.append((start, parity))
                    start += array.shape[0] // side
            at = start
        sums_shape = VMEM((blocks + 1, side, side), jnp.float32)
        out = kernel_call(
            functools.partial(stage_kernel, stage, first, layout),
            f"tiles_{stage}",
            1 + 2.0 * len(STAGES[stage]),
            out_shape=(sums_shape, sums_shape, VMEM((8, side), jnp.float32)),
            in_specs=[smem, smem, vmem, vmem] + [vmem] * len(points) + [hbm, hbm] + ([] if first else [vmem, vmem]),
            out_specs=(vmem, vmem, vmem),
            input_output_aliases={} if first else {6 + len(points): 0, 7 + len(points): 1},
            scratch_shapes=[
                VMEM((at, side, side), jnp.bfloat16),
                VMEM((at, side), jnp.float32),
                VMEM((2, GROUP, side, side), jnp.bfloat16),
                VMEM((GROUP, side, side), jnp.bfloat16),
                pltpu.SemaphoreType.DMA((2,)),
            ],
        )(place, lists, rows, norms, *points, targets, other_targets, *([] if first else sums))
        return out[:2], out[2]

    p20 = along_z(coords)
    p01 = along_y(coords)
    a10 = along_x(coords)
    near_rows = along_core(coords)
    p20, p01, a10, weights = gated((p20, p01, a10, weights))
    r10 = along_x(chosen(p01, p20))
    p40 = along_z(p20)
    p21 = along_y(p20)
    far_rows = along_core(p01)
    rows, norms = kernel_call(
        rows_kernel,
        "row_operands",
        3,
        out_shape=(VMEM((blocks, side, side), jnp.bfloat16), VMEM((blocks, side, side), jnp.float32)),
        in_specs=[smem] + [vmem] * 4,
        out_specs=(vmem, vmem),
    )(place, coords, near_rows, p01, far_rows)
    rows = pltpu.with_memory_space_constraint(rows, VMEM)
    norms = pltpu.with_memory_space_constraint(norms, VMEM)

    sums, token = tiles(0, None, (coords,), (p01,), (p20,))
    p40, p21, r10, a10, weights = gated((p40, p21, r10, a10, weights), token)
    p10 = chosen(r10, a10)
    p41 = along_y(p40)
    t21 = along_x(p21)
    p30 = along_z(p10)
    more_weights = along_core(weights)
    sums, token = tiles(1, sums, (p10,), (p21,), (p40,))
    p41, t21, p30, weights, more_weights = gated((p41, t21, p30, weights, more_weights), token)
    half = own_rows // 2
    d31 = along_x(p41[:half]), along_z(t21[half:])
    weights = weights + more_weights
    more_weights = along_y(weights)
    sums, token = tiles(2, sums, (p41,), (t21,), (p30,))
    *d31, weights, more_weights = gated((*d31, weights, more_weights), token)
    sums, token = tiles(3, sums, {1: d31, 0: (r10,)})
    scale = kernel_call(
        scale_kernel,
        "row_scale",
        1,
        out_shape=jax.ShapeDtypeStruct((own_rows, side), jnp.float32),
        in_specs=[smem, vmem],
        out_specs=vmem,
    )(place, weights + more_weights)

    def pack_core(flip, name, points):
        return kernel_call(
            functools.partial(pack_core_kernel, flip),
            name,
            1,
            out_shape=jax.ShapeDtypeStruct((own_rows, side), jnp.float32),
            in_specs=[smem] + [vmem] * 3,
            out_specs=vmem,
        )(place, *sums, points)

    got_far = along_core(pack_core(3, "pack_core_far", far_rows))
    to_far = kernel_call(
        pack_far_kernel,
        "pack_far",
        1.5,
        out_shape=jax.ShapeDtypeStruct((own_rows + count, side), jnp.bfloat16),
        in_specs=[smem] + [vmem] * 4,
        out_specs=vmem,
    )(place, *sums, got_far, p01)
    far = along_y(to_far)
    got_near = along_core(pack_core(1, "pack_core_near", near_rows))
    return kernel_call(
        finish_kernel,
        "finish",
        1.5,
        out_shape=jax.ShapeDtypeStruct((own_rows, width), jnp.float32),
        in_specs=[smem] + [vmem] * 6,
        out_specs=vmem,
    )(place, *sums, got_near, far, scale, coords)


def solution(mesh):
    in_specs = (
        P(("col", "rep"), None),
        P(("col", "rep"), None, None, None, None),
        P(("col", "rep"), None, None, None),
        P(("col", "rep"), None),
    )
    out_specs = P(("col", "rep"), None)
    return jax.shard_map(
        per_device, mesh=mesh, in_specs=in_specs, out_specs=out_specs, check_vma=False
    )
```

```python
import functools

import jax
import jax.numpy as jnp
from jax import lax
from jax.experimental import pallas as pl
from jax.experimental.pallas import tpu as pltpu
from jax.sharding import PartitionSpec as P

GROUP = 16
SUM_GROUP = 8
COST = 0.25
VMEM_LIMIT = 34 * 1024 * 1024
VMEM, SMEM, HBM = pltpu.VMEM, pltpu.SMEM, pltpu.HBM
STAGES = (
    ((0, 0), (1, 1), (4, 4)),
    ((2, 2), (5, 5), (8, 8)),
    ((9, 9), (3, 7), (6, 6)),
    ((7, 3),),
)


def place_of_device(stride):
    return lax.axis_index("rep"), lax.rem(lax.div(lax.axis_index("col"), stride), 2) == 0


def lanes_of(shape):
    return lax.broadcasted_iota(jnp.int32, shape, len(shape) - 1)


def diagonal(side):
    return lax.broadcasted_iota(jnp.int32, (side, side), 0) == lanes_of((side, side))


def row_of(column):
    return jnp.sum(jnp.where(diagonal(column.shape[0]), column, 0.0), axis=0, keepdims=True)


def column_of(row):
    return jnp.sum(jnp.where(diagonal(row.shape[1]), row, 0.0), axis=1, keepdims=True)


def lists_kernel(stride, per_quarter, codes, out):
    rep, even = place_of_device(stride)
    core, mine = rep & 1, lax.shift_right_arithmetic(rep, 1)
    offsets, width = codes.shape
    room = out.shape[1] - 128
    lanes = lanes_of((1, width))
    later = lax.broadcasted_iota(jnp.int32, (width, width), 0) <= lanes_of((width, width))
    later = jnp.where(later, 1.0, 0.0).astype(jnp.bfloat16)
    place_of = lax.broadcasted_iota(jnp.int32, (room, width), 0).astype(jnp.float32) + 1.0
    for stage, arrays in enumerate(STAGES):
        before = jnp.zeros((1, 1), jnp.float32)
        listed = jnp.zeros((32, room), jnp.float32)
        for offset in range(offsets):
            here = [(m, *pair) for m, pair in enumerate(arrays) if offset in (pair[0] // 2, pair[1] // 2)]
            if not here:
                continue
            code = codes[offset : offset + 1, :]
            row, col = lax.shift_right_arithmetic(code, 8), code & 255
            quarter = jnp.zeros_like(col)
            for edge in range(1, 4):
                quarter += jnp.where(col >= edge * per_quarter, 1, 0)
            match = jnp.zeros((1, width), jnp.float32)
            column = (col - quarter * per_quarter).astype(jnp.float32)
            for index, at_even, at_odd in here:
                piece = jnp.where(even, at_even, at_odd)
                wanted = jnp.bitwise_xor(mine, piece & 1) * 2 + core
                wanted = jnp.where(lax.shift_right_arithmetic(piece, 1) == offset, wanted, -1)
                hit = jnp.where((code >= 0) & (quarter == wanted), 1.0, 0.0)
                match += hit
                column += hit * (index * per_quarter)
            found = before + jnp.dot(
                jnp.broadcast_to(match, (16, width)).astype(jnp.bfloat16), later, preferred_element_type=jnp.float32
            )[0:1]
            before += jnp.sum(match, axis=1, keepdims=True)
            chosen = jnp.where((place_of == found) & (match > 0.0), 1.0, 0.0).astype(jnp.bfloat16)
            values = [lanes.astype(jnp.float32), row.astype(jnp.float32), column, jnp.full((1, width), offset, jnp.float32)]
            values = jnp.concatenate([jnp.broadcast_to(v, (8, width)) for v in values], axis=0).astype(jnp.bfloat16)
            listed += lax.dot_general(
                values, chosen, (((1,), (1,)), ((), ())), preferred_element_type=jnp.float32
            )
        listed = listed.astype(jnp.int32)
        lane, row, column, offset = listed[0:1], listed[8:9], listed[16:17], listed[24:25]
        slots = width // 2
        tile = offset * slots + lane + jnp.where(lane >= slots, (offsets - 1) * slots, 0)
        out[stage : stage + 1, :room] = tile * 65536 + row * 256 + column
        out[stage : stage + 1, room:] = jnp.broadcast_to(before.astype(jnp.int32), (1, 128))


def weights_kernel(codes, counts, targets, out, sums):
    step = pl.program_id(0)
    blocks, side = out.shape
    total = counts[step]

    @pl.when(step == 0)
    def _():
        sums[...] = jnp.zeros_like(sums)

    def visit(group, carry):
        for unit in range(SUM_GROUP):
            slot = group * SUM_GROUP + unit
            row = jnp.where(slot < total, lax.shift_right_arithmetic(codes[step, slot], 8), blocks)
            share = pltpu.reciprocal(targets[0, slot].astype(jnp.float32), approx=True)
            sums[row] += share * share
        return carry

    lax.fori_loop(0, (total + SUM_GROUP - 1) // SUM_GROUP, visit, 0)

    @pl.when(step == pl.num_programs(0) - 1)
    def _():
        def close(group, carry):
            for unit in range(8):
                whole = jnp.sum(sums[group * 8 + unit], axis=1, keepdims=True)
                out[pl.ds(group * 8 + unit, 1), :] = row_of(whole)
            return carry

        lax.fori_loop(0, blocks // 8, close, 0)


def scale_kernel(weights, more_weights, out):
    count = weights.shape[0] // 4
    side = weights.shape[1]
    own = pl.ds(pl.multiple_of(lax.axis_index("rep") * count, count), count)
    own = weights[own, :] + more_weights[own, :]
    for block in range(count):
        total = column_of(own[block : block + 1, :])
        out[block * side : (block + 1) * side, :] = jnp.broadcast_to(1.0 / (total + 1.0), (side, side))


def rows_kernel(q0, q1, q2, q3, out, norms):
    side = out.shape[1]
    count = q0.shape[0] // side
    for index, quarter in enumerate((q0, q1, q2, q3)):
        holder = jnp.bitwise_xor(lax.axis_index("rep"), index)

        def visit(block, carry, quarter=quarter, holder=holder):
            points = quarter[pl.ds(pl.multiple_of(block * side, side), side), :].astype(jnp.float32)
            out[holder * count + block] = (-2.0 * points).astype(jnp.bfloat16)
            norm = jnp.sum(points * points, axis=1, keepdims=True) + 1.0
            norms[holder * count + block] = jnp.broadcast_to(norm, (side, side))
            return carry

        lax.fori_loop(0, count, visit, 0, unroll=4)


def stage_kernel(stage, first, layout, stride, tokens, lists, rows, norms, *rest):
    parts = len(layout)
    points_refs, (own, other), rest = rest[:parts], rest[parts : parts + 2], rest[parts + 2 :]
    rest = rest[tokens:] if first else rest[tokens + 2 :]
    even = place_of_device(stride)[1]
    pulled, summed, token, right, column_norms, ring, ratios, sems = rest
    side = rows.shape[1]
    tiles = own.shape[0]
    dummy = pulled.shape[0] - 1
    total = lists[stage, lists.shape[1] - 1]
    groups = (total + GROUP - 1) // GROUP
    token[...] = jnp.zeros_like(token)

    def entry(index):
        return lists[stage, jnp.minimum(index, total - 1)]

    def fetch(group, slot):
        for unit in range(GROUP):
            tile = lax.shift_right_arithmetic(entry(group * GROUP + unit), 16)

            @pl.when(tile < tiles)
            def _():
                pltpu.make_async_copy(own.at[tile], ring.at[slot, unit], sems.at[slot]).start()

            @pl.when(tile >= tiles)
            def _():
                pltpu.make_async_copy(other.at[tile - tiles], ring.at[slot, unit], sems.at[slot]).start()

    @pl.when(groups > 0)
    def _():
        fetch(0, 0)

    if first:
        pulled[...] = jnp.zeros_like(pulled)
        summed[...] = jnp.zeros_like(summed)

    @pl.when(groups > 0)
    def _():
        for points_ref, (at, parity) in zip(points_refs, layout, strict=True):

            def build(block, carry, points_ref=points_ref, at=at):
                points = points_ref[pl.ds(pl.multiple_of(block * side, side), side), :]
                right[at + block] = points
                points = points.astype(jnp.float32)
                column_norms[pl.ds(at + block, 1), :] = row_of(jnp.sum(points * points, axis=1, keepdims=True))
                return carry

            held = points_ref.shape[0] // side // 4

            def build_four(four, carry, build=build):
                for unit in range(4):
                    build(four * 4 + unit, carry)
                return carry

            if parity is not None:
                held = jnp.where(even == (parity == 1), held, 0)
            lax.fori_loop(0, held, build_four, 0)

    def visit(group, carry):
        slot = lax.rem(group, 2)

        @pl.when(group + 1 < groups)
        def _():
            fetch(group + 1, 1 - slot)

        pltpu.make_async_copy(own.at[pl.ds(0, GROUP)], ring.at[slot], sems.at[slot]).wait()
        for unit in range(GROUP):
            code = entry(group * GROUP + unit)
            row, column = lax.shift_right_arithmetic(code, 8) & 255, code & 255
            square = lax.dot_general(
                rows[row], right[column], (((1,), (1,)), ((), ())), preferred_element_type=jnp.float32
            )
            square += norms[row] + column_norms[pl.ds(column, 1), :]
            share = pltpu.reciprocal(ring[slot, unit].astype(jnp.float32), approx=True)
            ratios[unit] = (share * (share - lax.rsqrt(square))).astype(jnp.bfloat16)
        for unit in range(GROUP):
            index = group * GROUP + unit
            code = entry(index)
            place = jnp.where(index < total, lax.shift_right_arithmetic(code, 8) & 255, dummy)
            pulled[place] += jnp.dot(ratios[unit], right[code & 255], preferred_element_type=jnp.float32)
            summed[place] += ratios[unit].astype(jnp.float32)
        return carry

    lax.fori_loop(0, groups, visit, 0)


def gate_kernel(*refs):
    pass


def halves_kernel(first, second, weights, more_weights, *rest):
    upper, lower, total = rest[-3:]
    half = upper.shape[0]
    upper[...] = first[:half, :]
    lower[...] = second[half:, :]
    total[...] = weights[...] + more_weights[...]


def choose_kernel(stride, at_even, at_odd, out):
    even = place_of_device(stride)[1]

    @pl.when(even)
    def _():
        out[...] = at_even[...]

    @pl.when(jnp.logical_not(even))
    def _():
        out[...] = at_odd[...]


def drift(pulled, summed, block, points):
    return pulled[block] - jnp.sum(summed[block], axis=1, keepdims=True) * points


def pack_core_kernel(flip, pulled, summed, points_ref, out):
    side = pulled.shape[1]
    count = (pulled.shape[0] - 1) // 4
    base = jnp.bitwise_xor(lax.axis_index("rep"), flip) * count
    for block in range(count):
        rows = slice(block * side, (block + 1) * side)
        out[rows, :] = drift(pulled, summed, base + block, points_ref[rows, :].astype(jnp.float32))


def pack_far_kernel(pulled, summed, norms, got, points_ref, out):
    side = pulled.shape[1]
    count = (pulled.shape[0] - 1) // 4
    base = jnp.bitwise_xor(lax.axis_index("rep"), 2) * count
    ones = jnp.ones((side, side), jnp.bfloat16)
    shares = []
    for block in range(count):
        rows = slice(block * side, (block + 1) * side)
        points = points_ref[rows, :].astype(jnp.float32)
        total = drift(pulled, summed, base + block, points) + got[rows, :]
        along = jnp.dot((total * points).astype(jnp.bfloat16), ones, preferred_element_type=jnp.float32)
        share = (along * pltpu.reciprocal(norms[base + block] - (1.0 - 1e-6), approx=True)).astype(jnp.bfloat16).astype(jnp.float32)
        out[rows, :] = (total - share * points).astype(jnp.bfloat16)
        shares.append(jnp.sum(jnp.where(diagonal(side), share, 0.0), axis=0, keepdims=True))
    out[count * side :, :] = jnp.concatenate(shares, axis=0).astype(jnp.bfloat16)


def base_kernel(pulled, summed, near, scale, points_ref, out):
    side = pulled.shape[1]
    count = (pulled.shape[0] - 1) // 4
    base = lax.axis_index("rep") * count
    for block in range(count):
        rows = slice(block * side, (block + 1) * side)
        points = points_ref[rows, :].astype(jnp.float32)
        total = drift(pulled, summed, base + block, points) + near[rows, :]
        out[rows, :] = points + scale[rows, :] * total


def finish_kernel(base, far, scale, points_ref, out):
    count, side = far.shape[0] - points_ref.shape[0], far.shape[1]
    shares = far[count * side :, :].astype(jnp.float32)
    for block in range(count):
        rows = slice(block * side, (block + 1) * side)
        points = points_ref[rows, :].astype(jnp.float32)
        total = far[rows, :].astype(jnp.float32) + column_of(shares[block : block + 1, :]) * points
        out[rows, :] = base[rows, :] + scale[rows, :] * total


def kernel_call(body, name, cost, **options):
    return pl.pallas_call(
        body,
        name=name,
        compiler_params=pltpu.CompilerParams(vmem_limit_bytes=VMEM_LIMIT),
        cost_estimate=pl.CostEstimate(
            flops=int(cost * COST * 1e9), bytes_accessed=int(cost * COST * 3e6), transcendentals=0
        ),
        **options,
    )


def per_device(coords, dissim, tile_blocks, tile_count):
    own_rows, width = coords.shape
    _, offsets, slots, side, _ = dissim.shape
    targets = dissim.reshape(offsets * slots, side, side)
    reps = lax.axis_size("rep")
    stride = lax.axis_size("col") // 8
    count = own_rows // side
    blocks = reps * count

    def sent(value, place):
        cols = lax.axis_size("col")
        pairs = []
        for col in range(cols):
            for r in range(reps):
                to_col, to_rep = place(col, r)
                pairs.append((col * reps + r, (to_col % cols) * reps + to_rep))
        return lax.ppermute(value, ("col", "rep"), pairs)

    def along_y(value):
        return sent(value, lambda col, r: (col, r ^ 2))

    def along_core(value):
        return sent(value, lambda col, r: (col, r ^ 1))

    def along_z(value):
        return sent(value, lambda col, r: (col + 2 * stride, r))

    def along_x(value):
        return sent(value, lambda col, r: (col + stride if (col // stride) % 2 == 0 else col - stride, r))

    vmem = pl.BlockSpec(memory_space=VMEM)
    smem = pl.BlockSpec(memory_space=SMEM)
    anywhere = pl.BlockSpec(memory_space=pl.ANY)

    codes = tile_blocks[0, :, :, 0] * 256 + tile_blocks[0, :, :, 1]
    alive = jnp.arange(slots, dtype=jnp.int32)[None, :] < tile_count[0][:, None]
    codes = jnp.where(alive, codes, -1)
    other_codes = along_core(codes)
    other_targets = along_core(targets)

    def gated(values, *tokens):
        return kernel_call(
            gate_kernel,
            "gate",
            0.3,
            out_shape=tuple(jax.ShapeDtypeStruct(v.shape, v.dtype) for v in values),
            in_specs=[anywhere] * (len(values) + len(tokens)),
            out_specs=(anywhere,) * len(values),
            input_output_aliases={i: i for i in range(len(values))},
        )(*values, *tokens)

    weights = kernel_call(
        weights_kernel,
        "row_weights",
        9,
        out_shape=jax.ShapeDtypeStruct((blocks, side), jnp.float32),
        grid=(offsets,),
        in_specs=[smem, smem, pl.BlockSpec((1, slots, side, side), lambda k: (k, 0, 0, 0))],
        out_specs=vmem,
        scratch_shapes=[VMEM((blocks + 1, side, side), jnp.float32)],
    )(codes, tile_count[0], pltpu.with_memory_space_constraint(dissim[0], HBM))
    lists = kernel_call(
        functools.partial(lists_kernel, stride, count),
        "sort_slots",
        2,
        out_shape=jax.ShapeDtypeStruct((len(STAGES), 2 * slots * (offsets - 1) + 128), jnp.int32),
        in_specs=[vmem],
        out_specs=vmem,
    )(jnp.concatenate([codes, other_codes], axis=1))
    def chosen(at_even, at_odd):
        return kernel_call(
            functools.partial(choose_kernel, stride),
            "choose",
            0.5,
            out_shape=VMEM(at_even.shape, at_even.dtype),
            in_specs=[vmem, vmem],
            out_specs=vmem,
        )(at_even, at_odd)

    def tiles(stage, sums, *places, tokens=()):
        first = sums is None
        points, layout, at = [], [], 0
        for choices in places:
            choices = [(None, choices)] if not isinstance(choices, dict) else list(choices.items())
            for parity, arrays in choices:
                start = at
                for array in arrays:
                    points.append(array)
                    layout.append((start, parity))
                    start += array.shape[0] // side
            at = start
        sums_shape = VMEM((blocks + 1, side, side), jnp.float32)
        out = kernel_call(
            functools.partial(stage_kernel, stage, first, layout, stride, len(tokens)),
            f"tiles_{stage}",
            1 + 2.0 * len(STAGES[stage]),
            out_shape=(sums_shape, sums_shape, VMEM((8, side), jnp.float32)),
            in_specs=[smem, vmem, vmem]
            + [vmem] * len(points)
            + [anywhere] * 2
            + [anywhere] * len(tokens)
            + ([] if first else [vmem, vmem]),
            out_specs=(vmem, vmem, vmem),
            input_output_aliases={} if first else {5 + len(points) + len(tokens) + i: i for i in range(2)},
            scratch_shapes=[
                VMEM((at, side, side), jnp.bfloat16),
                VMEM((at, side), jnp.float32),
                VMEM((2, GROUP, side, side), jnp.bfloat16),
                VMEM((GROUP, side, side), jnp.bfloat16),
                pltpu.SemaphoreType.DMA((2,)),
            ],
        )(lists, rows, norms, *points, targets, other_targets, *tokens, *([] if first else sums))
        return out[:2], out[2]

    p20 = along_z(coords)
    p01 = along_y(coords)
    a10 = along_x(coords)
    near_rows = along_core(coords)
    p20, p01, a10, weights = gated((p20, p01, a10, weights))
    r10 = along_x(chosen(p01, p20))
    p40 = along_z(p20)
    p21 = along_y(p20)
    far_rows = along_core(p01)
    rows, norms = kernel_call(
        rows_kernel,
        "row_operands",
        3,
        out_shape=(VMEM((blocks, side, side), jnp.bfloat16), VMEM((blocks, side, side), jnp.float32)),
        in_specs=[vmem] * 4,
        out_specs=(vmem, vmem),
    )(coords, near_rows, p01, far_rows)
    rows = pltpu.with_memory_space_constraint(rows, VMEM)
    norms = pltpu.with_memory_space_constraint(norms, VMEM)

    sums, token = tiles(0, None, (coords,), (p01,), (p20,))
    p40, p21, r10, a10, weights = gated((p40, p21, r10, a10, weights), token)
    p10 = chosen(r10, a10)
    p41 = along_y(p40)
    t21 = along_x(p21)
    p30 = along_z(p10)
    more_weights = along_core(weights)
    sums, token = tiles(1, sums, (p10,), (p21,), (p40,))
    half = jax.ShapeDtypeStruct((own_rows // 2, width), coords.dtype)
    upper, lower, weights = kernel_call(
        halves_kernel,
        "halves",
        0.5,
        out_shape=(half, half, jax.ShapeDtypeStruct(weights.shape, weights.dtype)),
        in_specs=[vmem] * 4 + [anywhere],
        out_specs=(vmem,) * 3,
    )(p41, t21, weights, more_weights, token)
    d31 = along_x(upper), along_z(lower)
    more_weights = along_y(weights)
    sums, token = tiles(2, sums, (p41,), (t21,), (p30,))
    sums, token = tiles(3, sums, {1: d31, 0: (r10,)}, tokens=(more_weights,))
    scale = kernel_call(
        scale_kernel,
        "row_scale",
        1,
        out_shape=jax.ShapeDtypeStruct((own_rows, side), jnp.float32),
        in_specs=[vmem, vmem],
        out_specs=vmem,
    )(weights, more_weights)

    sums = [pltpu.with_memory_space_constraint(value, VMEM) for value in sums]

    def pack_core(flip, name, points):
        return kernel_call(
            functools.partial(pack_core_kernel, flip),
            name,
            1,
            out_shape=jax.ShapeDtypeStruct((own_rows, side), jnp.float32),
            in_specs=[vmem] * 3,
            out_specs=vmem,
        )(*sums, points)

    got_far = along_core(pack_core(3, "pack_core_far", far_rows))
    to_far = kernel_call(
        pack_far_kernel,
        "pack_far",
        1.5,
        out_shape=jax.ShapeDtypeStruct((own_rows + count, side), jnp.bfloat16),
        in_specs=[vmem] * 5,
        out_specs=vmem,
    )(*sums, norms, got_far, p01)
    far = along_y(to_far)
    got_near = along_core(pack_core(1, "pack_core_near", near_rows))
    base = kernel_call(
        base_kernel,
        "own_rows",
        1.5,
        out_shape=jax.ShapeDtypeStruct((own_rows, side), jnp.float32),
        in_specs=[vmem] * 5,
        out_specs=vmem,
    )(*sums, got_near, scale, coords)
    return kernel_call(
        finish_kernel,
        "finish",
        1,
        out_shape=jax.ShapeDtypeStruct((own_rows, width), jnp.float32),
        in_specs=[vmem] * 4,
        out_specs=vmem,
    )(base, far, scale, coords)


def solution(mesh):
    in_specs = (
        P(("col", "rep"), None),
        P(("col", "rep"), None, None, None, None),
        P(("col", "rep"), None, None, None),
        P(("col", "rep"), None),
    )
    out_specs = P(("col", "rep"), None)
    return jax.shard_map(
        per_device, mesh=mesh, in_specs=in_specs, out_specs=out_specs, check_vma=False
    )
```

```python
import functools

import jax
import jax.numpy as jnp
from jax import lax
from jax.experimental import pallas as pl
from jax.experimental.pallas import tpu as pltpu
from jax.sharding import PartitionSpec as P

GROUP = 16
SUM_GROUP = 8
COST = 0.25
VMEM_LIMIT = 34 * 1024 * 1024
VMEM, SMEM, HBM = pltpu.VMEM, pltpu.SMEM, pltpu.HBM
ALL, FAR, NEAR = None, True, False
STAGES = (
    (((0, 0), (1, 1), (4, 4)), ALL),
    (((2, 2), (5, 5), (8, 8)), ALL),
    (((9, 9), (3, 7), (6, 6)), FAR),
    (((7, 3),), FAR),
    (((9, 9), (3, 7), (6, 6), (7, 3)), NEAR),
)


def place_of_device(stride):
    return lax.axis_index("rep"), lax.rem(lax.div(lax.axis_index("col"), stride), 2) == 0


def lanes_of(shape):
    return lax.broadcasted_iota(jnp.int32, shape, len(shape) - 1)


def diagonal(side):
    return lax.broadcasted_iota(jnp.int32, (side, side), 0) == lanes_of((side, side))


def split_three(value):
    high = value.astype(jnp.bfloat16)
    rest = value - high.astype(jnp.float32)
    middle = rest.astype(jnp.bfloat16)
    return high, middle, (rest - middle.astype(jnp.float32)).astype(jnp.bfloat16)


def row_of(column):
    return jnp.sum(jnp.where(diagonal(column.shape[0]), column, 0.0), axis=0, keepdims=True)


def column_of(row):
    return jnp.sum(jnp.where(diagonal(row.shape[1]), row, 0.0), axis=1, keepdims=True)


def lists_kernel(stride, per_quarter, codes, *outs):
    rep, even = place_of_device(stride)
    core, mine = rep & 1, lax.shift_right_arithmetic(rep, 1)
    offsets, width = codes.shape
    room = outs[0].shape[1] - 128
    lanes = lanes_of((1, width))
    later = lax.broadcasted_iota(jnp.int32, (width, width), 0) <= lanes_of((width, width))
    later = jnp.where(later, 1.0, 0.0).astype(jnp.bfloat16)
    place_of = lax.broadcasted_iota(jnp.int32, (room, width), 0).astype(jnp.float32) + 1.0
    for stage, (arrays, side_of_rows) in enumerate(STAGES):
        before = jnp.zeros((1, 1), jnp.float32)
        listed = jnp.zeros((32, room), jnp.float32)
        for offset in range(offsets):
            here = [(m, *pair) for m, pair in enumerate(arrays) if offset in (pair[0] // 2, pair[1] // 2)]
            if not here:
                continue
            code = codes[offset : offset + 1, :]
            row, col = lax.shift_right_arithmetic(code, 8), code & 255
            quarter, row_half = jnp.zeros_like(col), jnp.where(row >= 2 * per_quarter, 1, 0)
            for edge in range(1, 4):
                quarter += jnp.where(col >= edge * per_quarter, 1, 0)
            live = code >= 0
            if side_of_rows is not ALL:
                live = live & ((row_half != mine) if side_of_rows else (row_half == mine))
            match = jnp.zeros((1, width), jnp.float32)
            column = (col - quarter * per_quarter).astype(jnp.float32)
            for index, at_even, at_odd in here:
                piece = jnp.where(even, at_even, at_odd)
                wanted = jnp.bitwise_xor(mine, piece & 1) * 2 + core
                wanted = jnp.where(lax.shift_right_arithmetic(piece, 1) == offset, wanted, -1)
                hit = jnp.where(live & (quarter == wanted), 1.0, 0.0)
                match += hit
                column += hit * (index * per_quarter)
            found = before + jnp.dot(
                jnp.broadcast_to(match, (16, width)).astype(jnp.bfloat16), later, preferred_element_type=jnp.float32
            )[0:1]
            before += jnp.sum(match, axis=1, keepdims=True)
            chosen = jnp.where((place_of == found) & (match > 0.0), 1.0, 0.0).astype(jnp.bfloat16)
            values = [lanes.astype(jnp.float32), row.astype(jnp.float32), column, jnp.full((1, width), offset, jnp.float32)]
            values = jnp.concatenate([jnp.broadcast_to(v, (8, width)) for v in values], axis=0).astype(jnp.bfloat16)
            listed += lax.dot_general(
                values, chosen, (((1,), (1,)), ((), ())), preferred_element_type=jnp.float32
            )
        listed = listed.astype(jnp.int32)
        lane, row, column, offset = listed[0:1], listed[8:9], listed[16:17], listed[24:25]
        slots = width // 2
        tile = offset * slots + lane + jnp.where(lane >= slots, (offsets - 1) * slots, 0)
        outs[stage][:, :room] = tile * 65536 + row * 256 + column
        outs[stage][:, room:] = jnp.broadcast_to(before.astype(jnp.int32), (1, 128))


def weights_kernel(codes, counts, targets, out, sums):
    step = pl.program_id(0)
    blocks, side = out.shape
    total = counts[step]

    @pl.when(step == 0)
    def _():
        sums[...] = jnp.zeros_like(sums)

    def visit(group, carry):
        for unit in range(SUM_GROUP):
            slot = group * SUM_GROUP + unit
            row = jnp.where(slot < total, lax.shift_right_arithmetic(codes[step, slot], 8), blocks)
            share = pltpu.reciprocal(targets[0, slot].astype(jnp.float32), approx=True)
            sums[row] += share * share
        return carry

    lax.fori_loop(0, (total + SUM_GROUP - 1) // SUM_GROUP, visit, 0)

    @pl.when(step == pl.num_programs(0) - 1)
    def _():
        def close(group, carry):
            for unit in range(8):
                whole = jnp.sum(sums[group * 8 + unit], axis=1, keepdims=True)
                out[pl.ds(group * 8 + unit, 1), :] = row_of(whole)
            return carry

        lax.fori_loop(0, blocks // 8, close, 0)


def rows_kernel(q0, q1, q2, q3, out, norms):
    side = out.shape[1]
    count = q0.shape[0] // side
    for index, quarter in enumerate((q0, q1, q2, q3)):
        holder = jnp.bitwise_xor(lax.axis_index("rep"), index)

        def visit(block, carry, quarter=quarter, holder=holder):
            points = quarter[pl.ds(pl.multiple_of(block * side, side), side), :].astype(jnp.float32)
            out[holder * count + block] = (-2.0 * points).astype(jnp.bfloat16)
            norm = jnp.sum(points * points, axis=1, keepdims=True) + 1.0
            norms[holder * count + block] = jnp.broadcast_to(norm, (side, side))
            return carry

        lax.fori_loop(0, count, visit, 0, unroll=4)


def stage_kernel(first, layout, stride, tokens, lists, rows, norms, *rest):
    parts = len(layout)
    points_refs, (own, other), rest = rest[:parts], rest[parts : parts + 2], rest[parts + 2 :]
    rest = rest[tokens:] if first else rest[tokens + 2 :]
    even = place_of_device(stride)[1]
    pulled, summed, token, right, column_norms, ring, ratios, sems = rest
    side = rows.shape[1]
    tiles = own.shape[0]
    dummy = pulled.shape[0] - 1
    total = lists[0, lists.shape[1] - 1]
    groups = (total + GROUP - 1) // GROUP
    token[...] = jnp.zeros_like(token)

    def entry(index):
        return lists[0, jnp.minimum(index, total - 1)]

    def fetch(group, slot):
        for unit in range(GROUP):
            tile = lax.shift_right_arithmetic(entry(group * GROUP + unit), 16)

            @pl.when(tile < tiles)
            def _():
                pltpu.make_async_copy(own.at[tile], ring.at[slot, unit], sems.at[slot]).start()

            @pl.when(tile >= tiles)
            def _():
                pltpu.make_async_copy(other.at[tile - tiles], ring.at[slot, unit], sems.at[slot]).start()

    @pl.when(groups > 0)
    def _():
        fetch(0, 0)

    if first:
        pulled[...] = jnp.zeros_like(pulled)
        summed[...] = jnp.zeros_like(summed)

    @pl.when(groups > 0)
    def _():
        for points_ref, (at, parity) in zip(points_refs, layout, strict=True):

            def build(block, carry, points_ref=points_ref, at=at):
                points = points_ref[pl.ds(pl.multiple_of(block * side, side), side), :]
                right[at + block] = points
                points = points.astype(jnp.float32)
                column_norms[pl.ds(at + block, 1), :] = row_of(jnp.sum(points * points, axis=1, keepdims=True))
                return carry

            held = points_ref.shape[0] // side // 4

            def build_four(four, carry, build=build):
                for unit in range(4):
                    build(four * 4 + unit, carry)
                return carry

            if parity is not None:
                held = jnp.where(even == (parity == 1), held, 0)
            lax.fori_loop(0, held, build_four, 0)

    def visit(group, carry):
        slot = lax.rem(group, 2)

        @pl.when(group + 1 < groups)
        def _():
            fetch(group + 1, 1 - slot)

        pltpu.make_async_copy(own.at[pl.ds(0, GROUP)], ring.at[slot], sems.at[slot]).wait()
        for unit in range(GROUP):
            code = entry(group * GROUP + unit)
            row, column = lax.shift_right_arithmetic(code, 8) & 255, code & 255
            square = lax.dot_general(
                rows[row], right[column], (((1,), (1,)), ((), ())), preferred_element_type=jnp.float32
            )
            square += norms[row] + column_norms[pl.ds(column, 1), :]
            share = pltpu.reciprocal(ring[slot, unit].astype(jnp.float32), approx=True)
            ratios[unit] = (share * (share - lax.rsqrt(square))).astype(jnp.bfloat16)
        for unit in range(GROUP):
            index = group * GROUP + unit
            code = entry(index)
            place = jnp.where(index < total, lax.shift_right_arithmetic(code, 8) & 255, dummy)
            pulled[place] += jnp.dot(ratios[unit], right[code & 255], preferred_element_type=jnp.float32)
            summed[place] += ratios[unit].astype(jnp.float32)
        return carry

    lax.fori_loop(0, groups, visit, 0)


def gate_kernel(*refs):
    pass


def second_round_kernel(stride, weights, early, near, far, *refs):
    near_out, far_out, across = refs[-3:]
    even = place_of_device(stride)[1]
    near_out[...] = near[...]
    far_out[...] = far[...]

    @pl.when(even)
    def _():
        across[...] = near[...]

    @pl.when(jnp.logical_not(even))
    def _():
        across[...] = far[...]


def third_round_kernel(stride, at_even, at_odd, first, second, *refs):
    chosen, outs = refs[-5], refs[-4:]
    even = place_of_device(stride)[1]
    for index, whole in enumerate((first, second)):
        half = whole.shape[0] // 2
        outs[2 * index][...] = whole[:half, :]
        outs[2 * index + 1][...] = whole[half:, :]

    @pl.when(even)
    def _():
        chosen[...] = at_even[...]

    @pl.when(jnp.logical_not(even))
    def _():
        chosen[...] = at_odd[...]


def drift(pulled, summed, block, points):
    return pulled[block] - jnp.sum(summed[block], axis=1, keepdims=True) * points


def pack_core_kernel(flip, pulled, summed, points_ref, out):
    side = pulled.shape[1]
    count = (pulled.shape[0] - 1) // 4
    base = jnp.bitwise_xor(lax.axis_index("rep"), flip) * count
    for block in range(count):
        rows = slice(block * side, (block + 1) * side)
        out[rows, :] = drift(pulled, summed, base + block, points_ref[rows, :].astype(jnp.float32))


def pack_far_kernel(pulled, summed, norms, weights, more_weights, got, points_ref, out):
    side = pulled.shape[1]
    count = (pulled.shape[0] - 1) // 4
    base = jnp.bitwise_xor(lax.axis_index("rep"), 2) * count
    ones = jnp.ones((side, side), jnp.bfloat16)
    shares = []
    for block in range(count):
        rows = slice(block * side, (block + 1) * side)
        points = points_ref[rows, :].astype(jnp.float32)
        total = drift(pulled, summed, base + block, points) + got[rows, :]
        along = jnp.dot((total * points).astype(jnp.bfloat16), ones, preferred_element_type=jnp.float32)
        share = (along * pltpu.reciprocal(norms[base + block] - (1.0 - 1e-6), approx=True)).astype(jnp.bfloat16).astype(jnp.float32)
        out[rows, :] = (total - share * points).astype(jnp.bfloat16)
        shares.append(jnp.sum(jnp.where(diagonal(side), share, 0.0), axis=0, keepdims=True))
    at = count * side
    out[at : at + count, :] = jnp.concatenate(shares, axis=0).astype(jnp.bfloat16)
    theirs = pl.ds(pl.multiple_of(base, count), count)
    for part in split_three(weights[theirs, :] + more_weights[theirs, :]):
        at += count
        out[at : at + count, :] = part


def from_far_kernel(weights, more_weights, far, points_ref, out, scale):
    side = weights.shape[1]
    count = weights.shape[0] // 4
    at = count * side
    shares = far[at : at + count, :].astype(jnp.float32)
    own = pl.ds(pl.multiple_of(lax.axis_index("rep") * count, count), count)
    total_weights = weights[own, :] + more_weights[own, :]
    for part in range(1, 4):
        total_weights += far[at + part * count : at + (part + 1) * count, :].astype(jnp.float32)
    factors = 1.0 / (total_weights + 1.0)
    for block in range(count):
        rows = slice(block * side, (block + 1) * side)
        points = points_ref[rows, :].astype(jnp.float32)
        factor = jnp.broadcast_to(column_of(factors[block : block + 1, :]), (side, side))
        total = far[rows, :].astype(jnp.float32) + column_of(shares[block : block + 1, :]) * points
        scale[rows, :] = factor
        out[rows, :] = points + factor * total


def finish_kernel(moved, pulled, summed, near, scale, points_ref, out):
    side = pulled.shape[1]
    count = (pulled.shape[0] - 1) // 4
    base = lax.axis_index("rep") * count
    for block in range(count):
        rows = slice(block * side, (block + 1) * side)
        points = points_ref[rows, :].astype(jnp.float32)
        total = drift(pulled, summed, base + block, points) + near[rows, :]
        out[rows, :] = moved[rows, :] + scale[rows, :] * total


def kernel_call(body, name, cost, **options):
    return pl.pallas_call(
        body,
        name=name,
        compiler_params=pltpu.CompilerParams(vmem_limit_bytes=VMEM_LIMIT),
        cost_estimate=pl.CostEstimate(
            flops=int(cost * COST * 1e9), bytes_accessed=int(cost * COST * 3e6), transcendentals=0
        ),
        **options,
    )


def per_device(coords, dissim, tile_blocks, tile_count):
    own_rows, width = coords.shape
    _, offsets, slots, side, _ = dissim.shape
    targets = dissim.reshape(offsets * slots, side, side)
    reps = lax.axis_size("rep")
    stride = lax.axis_size("col") // 8
    count = own_rows // side
    blocks = reps * count

    def sent(value, place):
        cols = lax.axis_size("col")
        pairs = []
        for col in range(cols):
            for r in range(reps):
                to_col, to_rep = place(col, r)
                pairs.append((col * reps + r, (to_col % cols) * reps + to_rep))
        return lax.ppermute(value, ("col", "rep"), pairs)

    def along_y(value):
        return sent(value, lambda col, r: (col, r ^ 2))

    def along_core(value):
        return sent(value, lambda col, r: (col, r ^ 1))

    def along_z(value):
        return sent(value, lambda col, r: (col + 2 * stride, r))

    def along_x(value):
        return sent(value, lambda col, r: (col + stride if (col // stride) % 2 == 0 else col - stride, r))

    vmem = pl.BlockSpec(memory_space=VMEM)
    smem = pl.BlockSpec(memory_space=SMEM)
    anywhere = pl.BlockSpec(memory_space=pl.ANY)

    codes = tile_blocks[0, :, :, 0] * 256 + tile_blocks[0, :, :, 1]
    alive = jnp.arange(slots, dtype=jnp.int32)[None, :] < tile_count[0][:, None]
    codes = jnp.where(alive, codes, -1)
    other_codes = along_core(codes)
    other_targets = along_core(targets)

    def gated(values, *tokens):
        return kernel_call(
            gate_kernel,
            "gate",
            0.3,
            out_shape=tuple(jax.ShapeDtypeStruct(v.shape, v.dtype) for v in values),
            in_specs=[anywhere] * (len(values) + len(tokens)),
            out_specs=(anywhere,) * len(values),
            input_output_aliases={i: i for i in range(len(values))},
        )(*values, *tokens)

    weights = kernel_call(
        weights_kernel,
        "row_weights",
        9,
        out_shape=jax.ShapeDtypeStruct((blocks, side), jnp.float32),
        grid=(offsets,),
        in_specs=[smem, smem, pl.BlockSpec((1, slots, side, side), lambda k: (k, 0, 0, 0))],
        out_specs=vmem,
        scratch_shapes=[VMEM((blocks + 1, side, side), jnp.float32)],
    )(codes, tile_count[0], pltpu.with_memory_space_constraint(dissim[0], HBM))
    lists = kernel_call(
        functools.partial(lists_kernel, stride, count),
        "sort_slots",
        2,
        out_shape=(jax.ShapeDtypeStruct((1, 2 * slots * (offsets - 1) + 128), jnp.int32),) * len(STAGES),
        in_specs=[vmem],
        out_specs=(vmem,) * len(STAGES),
    )(jnp.concatenate([codes, other_codes], axis=1))
    def tiles(stage, sums, *places, tokens=()):
        first = sums is None
        points, layout, at = [], [], 0
        for choices in places:
            choices = [(None, choices)] if not isinstance(choices, dict) else list(choices.items())
            for parity, arrays in choices:
                start = at
                for array in arrays:
                    points.append(array)
                    layout.append((start, parity))
                    start += array.shape[0] // side
            at = start
        sums_shape = VMEM((blocks + 1, side, side), jnp.float32)
        out = kernel_call(
            functools.partial(stage_kernel, first, layout, stride, len(tokens)),
            f"tiles_{stage}",
            0.05 if STAGES[stage][1] is NEAR else 1 + 2.0 * len(STAGES[stage][0]),
            out_shape=(sums_shape, sums_shape, VMEM((8, side), jnp.float32)),
            in_specs=[smem, vmem, vmem]
            + [vmem] * len(points)
            + [anywhere] * 2
            + [anywhere] * len(tokens)
            + ([] if first else [vmem, vmem]),
            out_specs=(vmem, vmem, vmem),
            input_output_aliases={} if first else {5 + len(points) + len(tokens) + i: i for i in range(2)},
            scratch_shapes=[
                VMEM((at, side, side), jnp.bfloat16),
                VMEM((at, side), jnp.float32),
                VMEM((2, GROUP, side, side), jnp.bfloat16),
                VMEM((GROUP, side, side), jnp.bfloat16),
                pltpu.SemaphoreType.DMA((2,)),
            ],
        )(lists[stage], rows, norms, *points, targets, other_targets, *tokens, *([] if first else sums))
        return out[:2], out[2]

    p20 = along_z(coords)
    p01 = along_y(coords)
    a10 = along_x(coords)
    near_rows = along_core(coords)
    whole = jax.ShapeDtypeStruct((own_rows, width), coords.dtype)
    p01, p20, across = kernel_call(
        functools.partial(second_round_kernel, stride),
        "second_round",
        0.5,
        out_shape=(whole,) * 3,
        in_specs=[anywhere] * 2 + [vmem] * 2,
        out_specs=(vmem,) * 3,
    )(weights, a10, p01, p20)
    p40 = along_z(p20)
    p21 = along_y(p20)
    r10 = along_x(across)
    far_rows = along_core(p01)
    more_weights = along_core(weights)
    rows, norms = kernel_call(
        rows_kernel,
        "row_operands",
        3,
        out_shape=(VMEM((blocks, side, side), jnp.bfloat16), VMEM((blocks, side, side), jnp.float32)),
        in_specs=[vmem] * 4,
        out_specs=(vmem, vmem),
    )(coords, near_rows, p01, far_rows)
    rows = pltpu.with_memory_space_constraint(rows, VMEM)
    norms = pltpu.with_memory_space_constraint(norms, VMEM)

    sums, token = tiles(0, None, (coords,), (p01,), (p20,))
    half = jax.ShapeDtypeStruct((own_rows // 2, width), coords.dtype)
    p10, p21a, p21b, p40a, p40b = kernel_call(
        functools.partial(third_round_kernel, stride),
        "third_round",
        0.5,
        out_shape=(whole,) + (half,) * 4,
        in_specs=[vmem] * 4 + [anywhere] * 2,
        out_specs=(vmem,) * 5,
    )(r10, a10, p21, p40, more_weights, token)
    p41a = along_y(p40a)
    t21b = along_x(p21b)
    p30 = along_z(p10)
    p41b = along_y(p40b)
    t21a = along_x(p21a)
    sums, token = tiles(1, sums, (p10,), (p21,), (p40,))
    p41a, t21b = gated((p41a, t21b), token)
    d31 = along_x(p41a), along_z(t21b)
    last = {1: d31, 0: (r10,)}
    sums, token = tiles(2, sums, (p41a, p41b), (t21a, t21b), (p30,))
    sums, token = tiles(3, sums, last)
    def pack_core(flip, name, points):
        return kernel_call(
            functools.partial(pack_core_kernel, flip),
            name,
            1,
            out_shape=jax.ShapeDtypeStruct((own_rows, side), jnp.float32),
            in_specs=[vmem] * 3,
            out_specs=vmem,
        )(*sums, points)

    sums = [pltpu.with_memory_space_constraint(value, VMEM) for value in sums]
    got_far = along_core(pack_core(3, "pack_core_far", far_rows))
    to_far = kernel_call(
        pack_far_kernel,
        "pack_far",
        1.5,
        out_shape=jax.ShapeDtypeStruct((own_rows + 4 * count, side), jnp.bfloat16),
        in_specs=[vmem] * 7,
        out_specs=vmem,
    )(*sums, norms, weights, more_weights, got_far, p01)
    far = along_y(to_far)
    sums, token = tiles(4, sums, (p41a, p41b), (t21a, t21b), (p30,), last, tokens=(to_far,))
    sums = [pltpu.with_memory_space_constraint(value, VMEM) for value in sums]
    got_near = along_core(pack_core(1, "pack_core_near", near_rows))
    moved, scale = kernel_call(
        from_far_kernel,
        "from_far",
        80,
        out_shape=(jax.ShapeDtypeStruct((own_rows, side), jnp.float32),) * 2,
        in_specs=[vmem] * 4,
        out_specs=(vmem,) * 2,
    )(weights, more_weights, far, coords)
    return kernel_call(
        finish_kernel,
        "finish",
        1,
        out_shape=jax.ShapeDtypeStruct((own_rows, width), jnp.float32),
        in_specs=[vmem] * 6,
        out_specs=vmem,
    )(moved, *sums, got_near, scale, coords)


def solution(mesh):
    in_specs = (
        P(("col", "rep"), None),
        P(("col", "rep"), None, None, None, None),
        P(("col", "rep"), None, None, None),
        P(("col", "rep"), None),
    )
    out_specs = P(("col", "rep"), None)
    return jax.shard_map(
        per_device, mesh=mesh, in_specs=in_specs, out_specs=out_specs, check_vma=False
    )
```

```python
import functools

import jax
import jax.numpy as jnp
from jax import lax
from jax.experimental import pallas as pl
from jax.experimental.pallas import tpu as pltpu
from jax.sharding import PartitionSpec as P

GROUP = 16
SUM_GROUP = 8
COST = 0.25
VMEM_LIMIT = 34 * 1024 * 1024
VMEM, SMEM, HBM = pltpu.VMEM, pltpu.SMEM, pltpu.HBM
ALL, FAR, NEAR = None, True, False
STAGES = (
    (((0, 0), (1, 1), (4, 4)), ALL),
    (((2, 2), (5, 5), (8, 8)), ALL),
    (((9, 9), (3, 7), (6, 6)), FAR),
    (((7, 3),), FAR),
    (((9, 9), (3, 7), (6, 6), (7, 3)), NEAR),
)


def place_of_device(stride):
    return lax.axis_index("rep"), lax.rem(lax.div(lax.axis_index("col"), stride), 2) == 0


def lanes_of(shape):
    return lax.broadcasted_iota(jnp.int32, shape, len(shape) - 1)


def diagonal(side):
    return lax.broadcasted_iota(jnp.int32, (side, side), 0) == lanes_of((side, side))


def split_three(value):
    high = value.astype(jnp.bfloat16)
    rest = value - high.astype(jnp.float32)
    middle = rest.astype(jnp.bfloat16)
    return high, middle, (rest - middle.astype(jnp.float32)).astype(jnp.bfloat16)


def row_of(column):
    return jnp.sum(jnp.where(diagonal(column.shape[0]), column, 0.0), axis=0, keepdims=True)


def column_of(row):
    return jnp.sum(jnp.where(diagonal(row.shape[1]), row, 0.0), axis=1, keepdims=True)


def lists_kernel(stride, per_quarter, offsets, own, other, *outs):
    rep, even = place_of_device(stride)
    core, mine = rep & 1, lax.shift_right_arithmetic(rep, 1)
    width, tail = own.shape[1], pl.ds(other.shape[0] - own.shape[0], own.shape[0])
    slots = width // 2
    own, other = own[...].astype(jnp.float32), other[tail, :].astype(jnp.float32)
    first = lanes_of(own.shape) < slots
    all_rows = jnp.where(first, own, pltpu.roll(other, slots, axis=1)).astype(jnp.int32)
    all_columns = jnp.where(first, pltpu.roll(own, slots, axis=1), other).astype(jnp.int32)
    room = outs[0].shape[1] - 128
    lanes = lanes_of((1, width))
    later = lax.broadcasted_iota(jnp.int32, (width, width), 0) <= lanes_of((width, width))
    later = jnp.where(later, 1.0, 0.0).astype(jnp.bfloat16)
    place_of = lax.broadcasted_iota(jnp.int32, (room, width), 0).astype(jnp.float32) + 1.0
    for stage, (arrays, side_of_rows) in enumerate(STAGES):
        before = jnp.zeros((1, 1), jnp.float32)
        listed = jnp.zeros((32, room), jnp.float32)
        for offset in range(offsets):
            here = [(m, *pair) for m, pair in enumerate(arrays) if offset in (pair[0] // 2, pair[1] // 2)]
            if not here:
                continue
            row, col = all_rows[offset : offset + 1, :], all_columns[offset : offset + 1, :]
            quarter, row_half = jnp.zeros_like(col), jnp.where(row >= 2 * per_quarter, 1, 0)
            for edge in range(1, 4):
                quarter += jnp.where(col >= edge * per_quarter, 1, 0)
            live = row >= 0
            if side_of_rows is not ALL:
                live = live & ((row_half != mine) if side_of_rows else (row_half == mine))
            match = jnp.zeros((1, width), jnp.float32)
            column = (col - quarter * per_quarter).astype(jnp.float32)
            for index, at_even, at_odd in here:
                piece = jnp.where(even, at_even, at_odd)
                wanted = jnp.bitwise_xor(mine, piece & 1) * 2 + core
                wanted = jnp.where(lax.shift_right_arithmetic(piece, 1) == offset, wanted, -1)
                hit = jnp.where(live & (quarter == wanted), 1.0, 0.0)
                match += hit
                column += hit * (index * per_quarter)
            found = before + jnp.dot(
                jnp.broadcast_to(match, (16, width)).astype(jnp.bfloat16), later, preferred_element_type=jnp.float32
            )[0:1]
            before += jnp.sum(match, axis=1, keepdims=True)
            chosen = jnp.where((place_of == found) & (match > 0.0), 1.0, 0.0).astype(jnp.bfloat16)
            values = [lanes.astype(jnp.float32), row.astype(jnp.float32), column, jnp.full((1, width), offset, jnp.float32)]
            values = jnp.concatenate([jnp.broadcast_to(v, (8, width)) for v in values], axis=0).astype(jnp.bfloat16)
            listed += lax.dot_general(
                values, chosen, (((1,), (1,)), ((), ())), preferred_element_type=jnp.float32
            )
        listed = listed.astype(jnp.int32)
        lane, row, column, offset = listed[0:1], listed[8:9], listed[16:17], listed[24:25]
        tile = offset * slots + lane + jnp.where(lane >= slots, (offsets - 1) * slots, 0)
        outs[stage][:, :room] = tile * 65536 + row * 256 + column
        outs[stage][:, room:] = jnp.broadcast_to(before.astype(jnp.int32), (1, 128))


def weights_kernel(codes, counts, targets, out, sums):
    step = pl.program_id(0)
    blocks, side = out.shape
    total = counts[step]

    @pl.when(step == 0)
    def _():
        sums[...] = jnp.zeros_like(sums)

    def visit(group, carry):
        for unit in range(SUM_GROUP):
            slot = group * SUM_GROUP + unit
            row = jnp.where(slot < total, lax.shift_right_arithmetic(codes[step, slot], 8), blocks)
            share = pltpu.reciprocal(targets[0, slot].astype(jnp.float32), approx=True)
            sums[row] += share * share
        return carry

    lax.fori_loop(0, (total + SUM_GROUP - 1) // SUM_GROUP, visit, 0)

    @pl.when(step == pl.num_programs(0) - 1)
    def _():
        def close(group, carry):
            for unit in range(8):
                whole = jnp.sum(sums[group * 8 + unit], axis=1, keepdims=True)
                out[pl.ds(group * 8 + unit, 1), :] = row_of(whole)
            return carry

        lax.fori_loop(0, blocks // 8, close, 0)


def rows_kernel(count, own, partner, out, norms):
    side = out.shape[1]
    for index in range(4):
        holder = jnp.bitwise_xor(lax.axis_index("rep"), index)
        source, first = (own, partner)[index % 2], index // 2 * count

        def visit(block, carry, source=source, first=first, holder=holder):
            rows = pl.ds(pl.multiple_of((first + block) * side, side), side)
            points = source[rows, :].astype(jnp.float32)
            out[holder * count + block] = (-2.0 * points).astype(jnp.bfloat16)
            norm = jnp.sum(points * points, axis=1, keepdims=True) + 1.0
            norms[holder * count + block] = jnp.broadcast_to(norm, (side, side))
            return carry

        lax.fori_loop(0, count, visit, 0, unroll=4)


def stage_kernel(first, layout, stride, tokens, lists, rows, norms, *rest):
    parts = len(layout)
    points_refs, (own, other), rest = rest[:parts], rest[parts : parts + 2], rest[parts + 2 :]
    rest = rest[tokens:] if first else rest[tokens + 2 :]
    even = place_of_device(stride)[1]
    pulled, summed, token, right, column_norms, ring, ratios, sems = rest
    side = rows.shape[1]
    tiles = own.shape[0]
    dummy = pulled.shape[0] - 1
    total = lists[0, lists.shape[1] - 1]
    groups = (total + GROUP - 1) // GROUP
    token[...] = jnp.zeros_like(token)

    def entry(index):
        return lists[0, jnp.minimum(index, total - 1)]

    def fetch(group, slot):
        for unit in range(GROUP):
            tile = lax.shift_right_arithmetic(entry(group * GROUP + unit), 16)

            @pl.when(tile < tiles)
            def _():
                pltpu.make_async_copy(own.at[tile], ring.at[slot, unit], sems.at[slot]).start()

            @pl.when(tile >= tiles)
            def _():
                pltpu.make_async_copy(other.at[tile - tiles], ring.at[slot, unit], sems.at[slot]).start()

    @pl.when(groups > 0)
    def _():
        fetch(0, 0)

    if first:
        pulled[...] = jnp.zeros_like(pulled)
        summed[...] = jnp.zeros_like(summed)

    @pl.when(groups > 0)
    def _():
        for points_ref, (at, parity) in zip(points_refs, layout, strict=True):

            def build(block, carry, points_ref=points_ref, at=at):
                points = points_ref[pl.ds(pl.multiple_of(block * side, side), side), :]
                right[at + block] = points
                points = points.astype(jnp.float32)
                column_norms[pl.ds(at + block, 1), :] = row_of(jnp.sum(points * points, axis=1, keepdims=True))
                return carry

            held = points_ref.shape[0] // side // 4

            def build_four(four, carry, build=build):
                for unit in range(4):
                    build(four * 4 + unit, carry)
                return carry

            if parity is not None:
                held = jnp.where(even == (parity == 1), held, 0)
            lax.fori_loop(0, held, build_four, 0)

    def visit(group, carry):
        slot = lax.rem(group, 2)

        @pl.when(group + 1 < groups)
        def _():
            fetch(group + 1, 1 - slot)

        pltpu.make_async_copy(own.at[pl.ds(0, GROUP)], ring.at[slot], sems.at[slot]).wait()
        for unit in range(GROUP):
            code = entry(group * GROUP + unit)
            row, column = lax.shift_right_arithmetic(code, 8) & 255, code & 255
            square = lax.dot_general(
                rows[row], right[column], (((1,), (1,)), ((), ())), preferred_element_type=jnp.float32
            )
            square += norms[row] + column_norms[pl.ds(column, 1), :]
            share = pltpu.reciprocal(ring[slot, unit].astype(jnp.float32), approx=True)
            ratios[unit] = (share * (share - lax.rsqrt(square))).astype(jnp.bfloat16)
        for unit in range(GROUP):
            index = group * GROUP + unit
            code = entry(index)
            place = jnp.where(index < total, lax.shift_right_arithmetic(code, 8) & 255, dummy)
            pulled[place] += jnp.dot(ratios[unit], right[code & 255], preferred_element_type=jnp.float32)
            summed[place] += ratios[unit].astype(jnp.float32)
        return carry

    lax.fori_loop(0, groups, visit, 0)


def gate_kernel(*refs):
    pass


def second_round_kernel(weights, early, blocks_of, own, near, far, message, far_out):
    count = near.shape[0]
    message[:count, :] = own[...]
    message[count : 2 * count, :] = near[...]
    message[2 * count :, :] = blocks_of[...]
    far_out[...] = far[...]


def choose_kernel(stride, at_even, at_odd, out):
    even = place_of_device(stride)[1]

    @pl.when(even)
    def _():
        out[...] = at_even[pl.ds(out.shape[0], out.shape[0]), :]

    @pl.when(jnp.logical_not(even))
    def _():
        out[...] = at_odd[...]


def third_round_kernel(stride, at_even, at_odd, first, second, *refs):
    chosen, outs = refs[-5], refs[-4:]
    even = place_of_device(stride)[1]
    for index, whole in enumerate((first, second)):
        half = whole.shape[0] // 2
        outs[2 * index][...] = whole[:half, :]
        outs[2 * index + 1][...] = whole[half:, :]

    @pl.when(even)
    def _():
        chosen[...] = at_even[...]

    @pl.when(jnp.logical_not(even))
    def _():
        chosen[...] = at_odd[...]


def drift(pulled, summed, block, points):
    return pulled[block] - jnp.sum(summed[block], axis=1, keepdims=True) * points


def pack_core_kernel(flip, pulled, summed, points_ref, out):
    side = pulled.shape[1]
    count = (pulled.shape[0] - 1) // 4
    base = jnp.bitwise_xor(lax.axis_index("rep"), flip) * count
    for block in range(count):
        rows = slice(block * side, (block + 1) * side)
        points = points_ref[(flip // 2 * count + block) * side : (flip // 2 * count + block + 1) * side, :]
        out[rows, :] = drift(pulled, summed, base + block, points.astype(jnp.float32))


def pack_far_kernel(pulled, summed, norms, weights, more_weights, got, points_ref, out):
    side = pulled.shape[1]
    count = (pulled.shape[0] - 1) // 4
    base = jnp.bitwise_xor(lax.axis_index("rep"), 2) * count
    ones = jnp.ones((side, side), jnp.bfloat16)
    shares = []
    for block in range(count):
        rows = slice(block * side, (block + 1) * side)
        points = points_ref[rows, :].astype(jnp.float32)
        total = drift(pulled, summed, base + block, points) + got[rows, :]
        along = jnp.dot((total * points).astype(jnp.bfloat16), ones, preferred_element_type=jnp.float32)
        share = (along * pltpu.reciprocal(norms[base + block] - (1.0 - 1e-6), approx=True)).astype(jnp.bfloat16).astype(jnp.float32)
        out[rows, :] = (total - share * points).astype(jnp.bfloat16)
        shares.append(jnp.sum(jnp.where(diagonal(side), share, 0.0), axis=0, keepdims=True))
    at = count * side
    out[at : at + count, :] = jnp.concatenate(shares, axis=0).astype(jnp.bfloat16)
    theirs = pl.ds(pl.multiple_of(base, count), count)
    for part in split_three(weights[theirs, :] + more_weights[theirs, :]):
        at += count
        out[at : at + count, :] = part


def from_far_kernel(weights, more_weights, far, points_ref, out, scale):
    side = weights.shape[1]
    count = weights.shape[0] // 4
    at = count * side
    shares = far[at : at + count, :].astype(jnp.float32)
    own = pl.ds(pl.multiple_of(lax.axis_index("rep") * count, count), count)
    total_weights = weights[own, :] + more_weights[own, :]
    for part in range(1, 4):
        total_weights += far[at + part * count : at + (part + 1) * count, :].astype(jnp.float32)
    factors = 1.0 / (total_weights + 1.0)
    for block in range(count):
        rows = slice(block * side, (block + 1) * side)
        points = points_ref[rows, :].astype(jnp.float32)
        factor = jnp.broadcast_to(column_of(factors[block : block + 1, :]), (side, side))
        total = far[rows, :].astype(jnp.float32) + column_of(shares[block : block + 1, :]) * points
        scale[rows, :] = factor
        out[rows, :] = points + factor * total


def finish_kernel(moved, pulled, summed, near, scale, points_ref, out):
    side = pulled.shape[1]
    count = (pulled.shape[0] - 1) // 4
    base = lax.axis_index("rep") * count
    for block in range(count):
        rows = slice(block * side, (block + 1) * side)
        points = points_ref[rows, :].astype(jnp.float32)
        total = drift(pulled, summed, base + block, points) + near[rows, :]
        out[rows, :] = moved[rows, :] + scale[rows, :] * total


def kernel_call(body, name, cost, **options):
    return pl.pallas_call(
        body,
        name=name,
        compiler_params=pltpu.CompilerParams(vmem_limit_bytes=VMEM_LIMIT),
        cost_estimate=pl.CostEstimate(
            flops=int(cost * COST * 1e9), bytes_accessed=int(cost * COST * 3e6), transcendentals=0
        ),
        **options,
    )


def per_device(coords, dissim, tile_blocks, tile_count):
    own_rows, width = coords.shape
    _, offsets, slots, side, _ = dissim.shape
    targets = dissim.reshape(offsets * slots, side, side)
    reps = lax.axis_size("rep")
    stride = lax.axis_size("col") // 8
    count = own_rows // side
    blocks = reps * count

    def sent(value, place):
        cols = lax.axis_size("col")
        pairs = []
        for col in range(cols):
            for r in range(reps):
                to_col, to_rep = place(col, r)
                pairs.append((col * reps + r, (to_col % cols) * reps + to_rep))
        return lax.ppermute(value, ("col", "rep"), pairs)

    def along_y(value):
        return sent(value, lambda col, r: (col, r ^ 2))

    def along_core(value):
        return sent(value, lambda col, r: (col, r ^ 1))

    def along_z(value):
        return sent(value, lambda col, r: (col + 2 * stride, r))

    def along_x(value):
        return sent(value, lambda col, r: (col + stride if (col // stride) % 2 == 0 else col - stride, r))

    vmem = pl.BlockSpec(memory_space=VMEM)
    smem = pl.BlockSpec(memory_space=SMEM)
    anywhere = pl.BlockSpec(memory_space=pl.ANY)

    codes = tile_blocks[0, :, :, 0] * 256 + tile_blocks[0, :, :, 1]
    alive = jnp.arange(slots, dtype=jnp.int32)[None, :] < tile_count[0][:, None]
    codes = jnp.where(alive, codes, -1)
    blocks_of = jnp.concatenate([jnp.where(alive, tile_blocks[0, :, :, 0], -1), tile_blocks[0, :, :, 1]], axis=1)
    blocks_of = jnp.pad(blocks_of.astype(coords.dtype), ((0, 16 - offsets), (0, 0)))
    other_targets = along_core(targets)

    def gated(values, *tokens):
        return kernel_call(
            gate_kernel,
            "gate",
            0.3,
            out_shape=tuple(jax.ShapeDtypeStruct(v.shape, v.dtype) for v in values),
            in_specs=[anywhere] * (len(values) + len(tokens)),
            out_specs=(anywhere,) * len(values),
            input_output_aliases={i: i for i in range(len(values))},
        )(*values, *tokens)

    weights = kernel_call(
        weights_kernel,
        "row_weights",
        9,
        out_shape=jax.ShapeDtypeStruct((blocks, side), jnp.float32),
        grid=(offsets,),
        in_specs=[smem, smem, pl.BlockSpec((1, slots, side, side), lambda k: (k, 0, 0, 0))],
        out_specs=vmem,
        scratch_shapes=[VMEM((blocks + 1, side, side), jnp.float32)],
    )(codes, tile_count[0], pltpu.with_memory_space_constraint(dissim[0], HBM))
    p20 = along_z(coords)
    p01 = along_y(coords)
    a10 = along_x(coords)
    whole = jax.ShapeDtypeStruct((own_rows, width), coords.dtype)
    message, p20 = kernel_call(
        second_round_kernel,
        "second_round",
        0.5,
        out_shape=(jax.ShapeDtypeStruct((2 * own_rows + 16, width), coords.dtype), whole),
        in_specs=[anywhere] * 2 + [vmem] * 4,
        out_specs=(vmem,) * 2,
    )(weights, a10, blocks_of, coords, p01, p20)
    p40 = along_z(p20)
    p21 = along_y(p20)
    across = kernel_call(
        functools.partial(choose_kernel, stride),
        "choose",
        0.5,
        out_shape=whole,
        in_specs=[vmem] * 2,
        out_specs=vmem,
    )(message, p20)
    r10 = along_x(across)
    partner = along_core(message)
    more_weights = along_core(weights)
    lists = kernel_call(
        functools.partial(lists_kernel, stride, count, offsets),
        "sort_slots",
        2,
        out_shape=(jax.ShapeDtypeStruct((1, 2 * slots * (offsets - 1) + 128), jnp.int32),) * len(STAGES),
        in_specs=[vmem] * 2,
        out_specs=(vmem,) * len(STAGES),
    )(blocks_of, partner)
    def tiles(stage, sums, *places, tokens=()):
        first = sums is None
        points, layout, at = [], [], 0
        for choices in places:
            choices = [(None, choices)] if not isinstance(choices, dict) else list(choices.items())
            for parity, arrays in choices:
                start = at
                for array in arrays:
                    points.append(array)
                    layout.append((start, parity))
                    start += array.shape[0] // side
            at = start
        sums_shape = VMEM((blocks + 1, side, side), jnp.float32)
        out = kernel_call(
            functools.partial(stage_kernel, first, layout, stride, len(tokens)),
            f"tiles_{stage}",
            0.05 if STAGES[stage][1] is NEAR else 1 + 2.0 * len(STAGES[stage][0]),
            out_shape=(sums_shape, sums_shape, VMEM((8, side), jnp.float32)),
            in_specs=[smem, vmem, vmem]
            + [vmem] * len(points)
            + [anywhere] * 2
            + [anywhere] * len(tokens)
            + ([] if first else [vmem, vmem]),
            out_specs=(vmem, vmem, vmem),
            input_output_aliases={} if first else {5 + len(points) + len(tokens) + i: i for i in range(2)},
            scratch_shapes=[
                VMEM((at, side, side), jnp.bfloat16),
                VMEM((at, side), jnp.float32),
                VMEM((2, GROUP, side, side), jnp.bfloat16),
                VMEM((GROUP, side, side), jnp.bfloat16),
                pltpu.SemaphoreType.DMA((2,)),
            ],
        )(lists[stage], rows, norms, *points, targets, other_targets, *tokens, *([] if first else sums))
        return out[:2], out[2]
    rows, norms = kernel_call(
        functools.partial(rows_kernel, count),
        "row_operands",
        3,
        out_shape=(VMEM((blocks, side, side), jnp.bfloat16), VMEM((blocks, side, side), jnp.float32)),
        in_specs=[vmem] * 2,
        out_specs=(vmem, vmem),
    )(message, partner)
    rows = pltpu.with_memory_space_constraint(rows, VMEM)
    norms = pltpu.with_memory_space_constraint(norms, VMEM)

    sums, token = tiles(0, None, (coords,), (p01,), (p20,))
    half = jax.ShapeDtypeStruct((own_rows // 2, width), coords.dtype)
    p10, p21a, p21b, p40a, p40b = kernel_call(
        functools.partial(third_round_kernel, stride),
        "third_round",
        0.5,
        out_shape=(whole,) + (half,) * 4,
        in_specs=[vmem] * 4 + [anywhere] * 2,
        out_specs=(vmem,) * 5,
    )(r10, a10, p21, p40, more_weights, token)
    p41a = along_y(p40a)
    t21b = along_x(p21b)
    p30 = along_z(p10)
    p41b = along_y(p40b)
    t21a = along_x(p21a)
    sums, token = tiles(1, sums, (p10,), (p21,), (p40,))
    p41a, t21b = gated((p41a, t21b), token)
    d31 = along_x(p41a), along_z(t21b)
    last = {1: d31, 0: (r10,)}
    sums, token = tiles(2, sums, (p41a, p41b), (t21a, t21b), (p30,))
    sums, token = tiles(3, sums, last)
    def pack_core(flip, name, points):
        return kernel_call(
            functools.partial(pack_core_kernel, flip),
            name,
            1,
            out_shape=jax.ShapeDtypeStruct((own_rows, side), jnp.float32),
            in_specs=[vmem] * 3,
            out_specs=vmem,
        )(*sums, points)

    sums = [pltpu.with_memory_space_constraint(value, VMEM) for value in sums]
    got_far = along_core(pack_core(3, "pack_core_far", partner))
    to_far = kernel_call(
        pack_far_kernel,
        "pack_far",
        1.5,
        out_shape=jax.ShapeDtypeStruct((own_rows + 4 * count, side), jnp.bfloat16),
        in_specs=[vmem] * 7,
        out_specs=vmem,
    )(*sums, norms, weights, more_weights, got_far, p01)
    far = along_y(to_far)
    sums, token = tiles(4, sums, (p41a, p41b), (t21a, t21b), (p30,), last, tokens=(to_far,))
    sums = [pltpu.with_memory_space_constraint(value, VMEM) for value in sums]
    got_near = along_core(pack_core(1, "pack_core_near", partner))
    moved, scale = kernel_call(
        from_far_kernel,
        "from_far",
        80,
        out_shape=(jax.ShapeDtypeStruct((own_rows, side), jnp.float32),) * 2,
        in_specs=[vmem] * 4,
        out_specs=(vmem,) * 2,
    )(weights, more_weights, far, coords)
    return kernel_call(
        finish_kernel,
        "finish",
        1,
        out_shape=jax.ShapeDtypeStruct((own_rows, width), jnp.float32),
        in_specs=[vmem] * 6,
        out_specs=vmem,
    )(moved, *sums, got_near, scale, coords)


def solution(mesh):
    in_specs = (
        P(("col", "rep"), None),
        P(("col", "rep"), None, None, None, None),
        P(("col", "rep"), None, None, None),
        P(("col", "rep"), None),
    )
    out_specs = P(("col", "rep"), None)
    return jax.shard_map(
        per_device, mesh=mesh, in_specs=in_specs, out_specs=out_specs, check_vma=False
    )
```
